128 devices in a mesh: ep: 16 (over x, z), tp: 8 (over y, core).
Axes of the slice: x: 4, y: 4, z: 4, core: 2. Of those that a mesh axis runs over, the one named last changes fastest.
Arguments:
- tokens: bfloat16 [2048, 4096], P('ep', 'tp'), may hold values from -6 to 6
- out_grad: bfloat16 [2048, 4096], P('ep', 'tp'), may hold values from -6 to 6
- routes: int32 [2048, 4], P('ep'), may hold values from 0 to 15, all different within a row; in each aligned block of 128 rows (0 to 127, 128 to 255, ...) at most 64 rows name the same one
- probs: bfloat16 [2048, 4], P('ep'), may hold values from 0.019897461 to 0.59765625
- w_in: bfloat16 [16, 2, 1536, 4096], P('ep', None, 'tp'), as said below
- w_out: bfloat16 [16, 1536, 4096], P('ep', 'tp'), as said below
Outputs:
- in_grad: bfloat16 [2048, 4096], P('ep', 'tp')
- grad_in: bfloat16 [16, 2, 1536, 4096], P('ep', None, 'tp')
- grad_out: bfloat16 [16, 1536, 4096], P('ep', 'tp')
The draws below stay inside these ranges and needn't reach their ends.
Inputs may be any that keep to these rules, and one draw needn't show every extreme that they name: `routes`: each token names 4 different copies; within the tokens of one device (aligned blocks of 128 tokens) no copy is named more than 64 times, a bound that some block reaches. `w_in`: copies c and c + 8 hold equal weights. `w_out`: copies c and c + 8 hold equal weights.
All inputs are finite; a program needn't handle non-finite values.
Results may differ from the reference program's by a relative error of at most 0.02.
Values may be sent and summed in bfloat16 or wider, within the bound.
A program may use at most 128 MiB of HBM per device.

```python
import math
import jax
import jax.numpy as jnp
import numpy as np
from jax import lax

D = 4096
FF = 1536
TOP = 4
TOK_DEV = 128
COPIES = 16
EXPERTS = 8
CAP = 64
TOKENS = 2048
N_EP = 16
N_TP = 8


def draw_w_in(key, part):
    base = jax.random.normal(key, (EXPERTS, 2, FF, D), jnp.float32) * (1.0 / D ** 0.5)
    return jnp.concatenate([base, base], axis=0).astype(jnp.bfloat16)


def draw_w_out(key, part):
    base = jax.random.normal(jax.random.fold_in(key, 7), (EXPERTS, FF, D), jnp.float32) * (1.0 / FF ** 0.5)
    return jnp.concatenate([base, base], axis=0).astype(jnp.bfloat16)


def level_of(rng, extent, cuts, least, largest):
    gain = 1.0
    for dim, blocks in cuts:
        heights = jax.random.uniform(jax.random.fold_in(jax.random.fold_in(rng, 6), dim), (blocks,), jnp.float32, least / len(cuts), largest / len(cuts))
        gain = gain * jnp.repeat(jnp.exp(heights), extent[dim] // blocks).reshape((-1,) + (1,) * (len(extent) - 1 - dim))
    return gain


def deal_out(own_key, own, number, rows, count, top, reach, lean):
    ranking = jax.random.permutation(own_key, count)
    heavy_load, usual = shares(count, rows * top, reach, lean, True), shares(count, rows * top, reach, lean, False)
    places = jnp.arange(count)

    def named(tallies, offset_by):
        used = int((tallies > 0).sum())
        fixed = max(1, used // 4)
        shifted = fixed + (places - fixed + offset_by * (used - fixed)) % max(1, count - fixed)
        return jnp.zeros((count,), jnp.int32).at[ranking[jnp.where(places < fixed, places, shifted)]].set(jnp.asarray(tallies, jnp.int32))

    tallies = jnp.where(number % 4 == 0, named(heavy_load, number // 4), named(usual, number - number // 4 - 1))
    mixed = jax.random.permutation(jax.random.fold_in(own, 3), count)
    giver, receiver = mixed[0:count // 2 * 2:2], mixed[1:count // 2 * 2:2]
    margin = jnp.minimum(tallies[giver] - 1, reach - tallies[receiver]) // 2
    margin = jnp.where((giver == ranking[0]) | (receiver == ranking[0]) | (tallies[receiver] == 0), 0, jnp.maximum(margin, 0))
    shifted = jax.random.randint(jax.random.fold_in(own, 4), (count // 2,), 0, 1 << 20) % (margin + 1)
    tallies = tallies.at[giver].add(-shifted).at[receiver].add(shifted)
    members = jnp.searchsorted(jnp.cumsum(tallies), jnp.arange(rows * top), side="right").astype(jnp.int32)
    listing = members.reshape(top, rows).T
    listing = listing[jax.random.permutation(jax.random.fold_in(own, 1), rows)]
    offset_by = jax.random.randint(jax.random.fold_in(own, 2), (rows, 1), 0, top)
    return jnp.take_along_axis(listing, (jnp.arange(top)[None, :] + offset_by) % top, axis=1)


def shares(number_of, total, most, skew, full):
    loads = [(1 << 20) // math.isqrt(rank ** skew) + 1 for rank in range(1, number_of + 1)]
    largest = most if full else min(most, max(-(-total // number_of), total * loads[0] // sum(loads)))
    least = 1 if total - largest >= number_of - 1 else 0
    given, surplus = [largest] + [least] * (number_of - 1), total - largest - least * (number_of - 1)
    while surplus > 0:
        movable = [i for i in range(1, number_of) if given[i] < largest] or [i for i in range(1, number_of) if given[i] < most]
        whole, budget = sum([loads[i] for i in movable]), surplus
        for i in movable:
            addition = min(most - given[i], max(1, budget * loads[i] // whole), surplus)
            given[i] = given[i] + addition
            surplus = surplus - addition
    return np.array(given)


def bell_draw(stream_key, dims, deviation, most, shards=(), kind=jnp.bfloat16):
    drawn = deviation * jax.random.normal(stream_key, dims, jnp.float32)
    if shards:
        drawn = drawn * level_of(stream_key, dims, shards, -0.22, 0.18)
    return jnp.clip(drawn, -most, most).astype(kind)


def setup_inputs(seed: int = 0) -> dict:
    keys = jax.random.split(jax.random.key(seed), 7)
    tokens = bell_draw(keys[0], (TOKENS, D), 1.0, 6.0, ((0, 16), (1, 8)))
    out_grad = bell_draw(keys[1], (TOKENS, D), 1.0, 6.0, ((0, 16), (1, 8)))
    routes_keys = jax.random.split(jax.random.fold_in(keys[2], 1), TOKENS // TOK_DEV)
    routes_turns = jax.random.permutation(jax.random.fold_in(keys[2], 3), TOKENS // TOK_DEV)
    routes = jax.vmap(lambda own, number: deal_out(jax.random.fold_in(keys[2], 2), own, number, TOK_DEV, COPIES, TOP, CAP, 2))(routes_keys, routes_turns).reshape((TOKENS, TOP))
    probs = jnp.clip(jnp.exp(math.log(0.59765625) - 3.4024236 * jax.random.uniform(keys[3], (TOKENS, TOP), jnp.float32) ** level_of(keys[3], (TOKENS, TOP), ((0, 16),), -0.2, 0.2)), 0.019897461, 0.59765625).astype(jnp.bfloat16)
    w_in = draw_w_in(jax.random.fold_in(keys[6], 71), 0)
    w_out = draw_w_out(jax.random.fold_in(keys[6], 71), 0)
    return {"tokens": tokens, "out_grad": out_grad, "routes": routes, "probs": probs, "w_in": w_in, "w_out": w_out}


def slot_tables(block_routes, copies, cap):
    flat = block_routes.reshape(-1).astype(jnp.int32)
    nrows = flat.shape[0]
    onehot = (flat[:, None] == jnp.arange(copies, dtype=jnp.int32)[None, :]).astype(jnp.int32)
    ranks = jnp.sum((jnp.cumsum(onehot, axis=0) - 1) * onehot, axis=1)
    slot = (flat * cap + ranks).astype(jnp.int32)
    source = jnp.full((copies * cap,), nrows, jnp.int32).at[slot].set(jnp.arange(nrows, dtype=jnp.int32))
    return slot, source


def reference(tokens, out_grad, routes, probs, w_in, w_out):
    nrows = TOK_DEV * TOP
    blocks = routes.reshape(N_EP, TOK_DEV, TOP)
    slots, sources = jax.vmap(lambda b: slot_tables(b, COPIES, CAP))(blocks)
    per_copy_src = sources.reshape(N_EP, COPIES, CAP).transpose(1, 0, 2)
    probs_flat = probs.reshape(N_EP, nrows)
    contract_last = (((1,), (1,)), ((), ()))
    contract_rows = (((0,), (0,)), ((), ()))

    def one_copy(args):
        src, weights_in, weights_out = args
        valid = src < nrows
        local = jnp.minimum(src, nrows - 1).astype(jnp.int32)
        tok = (jnp.arange(N_EP, dtype=jnp.int32)[:, None] * TOK_DEV + local // TOP).astype(jnp.int32)
        scale = jnp.where(valid, jnp.take_along_axis(probs_flat, local, axis=1).astype(jnp.float32), 0.0)
        rows_x = jnp.where(valid[..., None], tokens[tok], jnp.zeros((), jnp.bfloat16)).reshape(N_EP * CAP, D)
        rows_g = (scale[..., None] * out_grad[tok].astype(jnp.float32)).astype(jnp.bfloat16).reshape(N_EP * CAP, D)
        w_gate = weights_in[0]
        w_up = weights_in[1]
        a = lax.dot_general(rows_x, w_gate, contract_last, preferred_element_type=jnp.float32)
        b = lax.dot_general(rows_x, w_up, contract_last, preferred_element_type=jnp.float32)
        sig = jax.nn.sigmoid(a)
        silu = a * sig
        hidden = (silu * b).astype(jnp.bfloat16)
        dh = lax.dot_general(rows_g, weights_out, contract_last, preferred_element_type=jnp.float32)
        da = (dh * b * sig * (1.0 + a * (1.0 - sig))).astype(jnp.bfloat16)
        db = (dh * silu).astype(jnp.bfloat16)
        ffl = FF // N_TP
        da_t = da.astype(jnp.float32).reshape(N_EP * CAP, N_TP, ffl)
        db_t = db.astype(jnp.float32).reshape(N_EP * CAP, N_TP, ffl)
        wg_t = w_gate.astype(jnp.float32).reshape(N_TP, ffl, D)
        wu_t = w_up.astype(jnp.float32).reshape(N_TP, ffl, D)
        parts = jnp.einsum("rtf,tfd->trd", da_t, wg_t) + jnp.einsum("rtf,tfd->trd", db_t, wu_t)
        row_grad = jnp.sum(parts.astype(jnp.bfloat16).astype(jnp.float32), axis=0).astype(jnp.bfloat16)
        own_in = jnp.stack([
            lax.dot_general(da, rows_x, contract_rows, preferred_element_type=jnp.float32),
            lax.dot_general(db, rows_x, contract_rows, preferred_element_type=jnp.float32)]).astype(jnp.bfloat16)
        own_out = lax.dot_general(hidden, rows_g, contract_rows, preferred_element_type=jnp.float32).astype(jnp.bfloat16)
        return row_grad.reshape(N_EP, CAP, D), own_in, own_out

    row_grads, own_in, own_out = lax.map(one_copy, (per_copy_src, w_in, w_out))
    by_source = row_grads.transpose(1, 0, 2, 3).reshape(N_EP, COPIES * CAP, D)
    picked = jnp.take_along_axis(by_source, slots[..., None], axis=1)
    in_grad = jnp.sum(picked.astype(jnp.float32).reshape(N_EP, TOK_DEV, TOP, D), axis=2).astype(jnp.bfloat16).reshape(TOKENS, D)
    grad_in = (own_in.astype(jnp.float32) + jnp.roll(own_in, EXPERTS, axis=0).astype(jnp.float32)).astype(jnp.bfloat16)
    grad_out = (own_out.astype(jnp.float32) + jnp.roll(own_out, EXPERTS, axis=0).astype(jnp.float32)).astype(jnp.bfloat16)
    return in_grad, grad_in, grad_out
```

```python
import jax
import jax.numpy as jnp
from jax import lax
from jax.sharding import PartitionSpec as P


def partner(block, axis, apart):
    count = lax.axis_size(axis)
    route = []
    for low in range(count):
        high = low | 1 << apart
        if high != low and high < count:
            route += [(low, high), (high, low)]
    return lax.ppermute(block, axis, route)


def slot_tables(block_routes, copies, cap):
    flat = block_routes.reshape(-1)
    nrows = flat.shape[0]
    before = jnp.arange(nrows, dtype=jnp.int32)
    earlier = (before[None, :] < before[:, None]) & (flat[None, :] == flat[:, None])
    ranks = jnp.sum(earlier.astype(jnp.int32), axis=1)
    slot = flat * cap + ranks
    source = (
        jnp.full((copies * cap,), nrows, jnp.int32).at[slot].set(jnp.arange(nrows, dtype=jnp.int32))
    )
    return (slot, source)


def body(tokens, out_grad, routes, probs, w_in, w_out):
    n_ep = lax.axis_size("ep")
    tok_dev, top = routes.shape
    nrows = tok_dev * top
    cap = 2 * nrows // n_ep
    slot, source = slot_tables(routes, n_ep, cap)
    valid = source < nrows
    local = jnp.minimum(source, nrows - 1)
    tok_index = local // top
    scale = jnp.where(valid, probs.reshape(-1)[local].astype(jnp.float32), 0.0)[:, None]
    packed_x = jnp.where(valid[:, None], tokens[tok_index], jnp.zeros((), jnp.bfloat16))
    packed_g = (scale * out_grad[tok_index].astype(jnp.float32)).astype(jnp.bfloat16)
    part = tokens.shape[1]
    send_x = packed_x.reshape(n_ep, cap, part)
    send_g = packed_g.reshape(n_ep, cap, part)
    recv_x, recv_g = (
        lax.all_to_all(send_x, "ep", split_axis=0, concat_axis=0, tiled=True),
        lax.all_to_all(send_g, "ep", split_axis=0, concat_axis=0, tiled=True),
    )
    rows_x = lax.all_gather(recv_x.reshape(n_ep * cap, part), "tp", axis=1, tiled=True)
    rows_g = lax.all_gather(recv_g.reshape(n_ep * cap, part), "tp", axis=1, tiled=True)
    width = rows_x.shape[1]
    w_gate = w_in[0, 0]
    w_up = w_in[0, 1]
    w_down = w_out[0]
    contract_last = (((1,), (1,)), ((), ()))
    a = lax.dot_general(rows_x, w_gate, contract_last, preferred_element_type=jnp.float32)
    b = lax.dot_general(rows_x, w_up, contract_last, preferred_element_type=jnp.float32)
    sig = jax.nn.sigmoid(a)
    silu = a * sig
    hidden = (silu * b).astype(jnp.bfloat16)
    dh = lax.dot_general(rows_g, w_down, contract_last, preferred_element_type=jnp.float32)
    da = (dh * b * sig * (1.0 + a * (1.0 - sig))).astype(jnp.bfloat16)
    db = (dh * silu).astype(jnp.bfloat16)
    partial_rows = jnp.dot(da, w_gate, preferred_element_type=jnp.float32)
    partial_rows = partial_rows + jnp.dot(db, w_up, preferred_element_type=jnp.float32)
    summed = lax.psum_scatter(
        partial_rows.reshape(n_ep, cap, width).astype(jnp.bfloat16),
        "tp",
        scatter_dimension=2,
        tiled=True,
    )
    back = lax.all_to_all(summed, "ep", split_axis=0, concat_axis=0, tiled=True)
    picked = back.reshape(n_ep * cap, back.shape[2])[slot]
    in_grad = jnp.sum(
        picked.astype(jnp.float32).reshape(tok_dev, top, back.shape[2]), axis=1
    ).astype(jnp.bfloat16)
    contract_rows = (((0,), (0,)), ((), ()))
    own_in = jnp.stack(
        [
            lax.dot_general(da, rows_x, contract_rows, preferred_element_type=jnp.float32),
            lax.dot_general(db, rows_x, contract_rows, preferred_element_type=jnp.float32),
        ]
    ).astype(jnp.bfloat16)[None]
    own_out = lax.dot_general(
        hidden, rows_g, contract_rows, preferred_element_type=jnp.float32
    ).astype(jnp.bfloat16)[None]
    half_bit = n_ep.bit_length() - 2
    other_in, other_out = partner((own_in, own_out), "ep", half_bit)
    grad_in = (own_in.astype(jnp.float32) + other_in.astype(jnp.float32)).astype(jnp.bfloat16)
    grad_out = (own_out.astype(jnp.float32) + other_out.astype(jnp.float32)).astype(jnp.bfloat16)
    return (in_grad, grad_in, grad_out)


def solution(mesh):
    return jax.shard_map(
        body,
        mesh=mesh,
        in_specs=(
            P("ep", "tp"),
            P("ep", "tp"),
            P("ep", None),
            P("ep", None),
            P("ep", None, "tp", None),
            P("ep", "tp", None),
        ),
        out_specs=(P("ep", "tp"), P("ep", None, "tp", None), P("ep", "tp", None)),
        check_vma=False,
    )
```

```python
import functools

import jax
import jax.numpy as jnp
from jax import lax
from jax.experimental import pallas as pl
from jax.experimental.pallas import tpu as pltpu
from jax.sharding import PartitionSpec as P

BF16 = jnp.bfloat16
F32 = jnp.float32
LAST = (((1,), (1,)), ((), ()))
FIRST = (((0,), (0,)), ((), ()))
ROWS = (((1,), (0,)), ((), ()))


def dot(a, b, dims):
    return lax.dot_general(a, b, dims, preferred_element_type=F32)


def kernel(
    n_ep,
    n_y,
    tok,
    og,
    routes,
    probs,
    w_in,
    w_out,
    in_grad,
    grad_in,
    grad_out,
    xs,
    gs,
    wi,
    wo,
    pack_x,
    pack_g,
    onehot,
    named,
    rank,
    share,
    ab,
    dh,
    hid,
    dadb_t,
    dadb,
    own_out,
    rec_out,
    own_in,
    rec_in,
    part_sib,
    part_rec,
    part,
    half_rec,
    full_rec,
    back,
    w_sem,
    a_send,
    a_recv,
    ring_send,
    core_send,
    g_recv,
    eo_send,
    eo_recv,
    ei_send,
    ei_recv,
    p_send,
    p_recv,
    h_send,
    h_recv,
    f_send,
    f_recv,
    b_send,
    b_recv,
    o_sem,
):
    rows, width = xs.shape[1], xs.shape[2]
    cap = rows // n_ep
    half = rows // 2
    ntok = tok.shape[0]
    ff = wo.shape[0]
    tile = min(256, rows)
    lane = min(128, rows)
    wide = min(256, width)
    e = lax.axis_index("ep")
    t = lax.axis_index("tp")
    y = t // 2
    core = t % 2
    sib = y * 2 + (1 - core)
    y_up = lax.rem(y + 1, n_y)
    y_far = lax.rem(y + 2, n_y)
    y_dn = lax.rem(y + n_y - 1, n_y)
    up, far, dn = (v * 2 + core for v in (y_up, y_far, y_dn))
    sup, sfar, sdn = (v * 2 + (1 - core) for v in (y_up, y_far, y_dn))
    other = lax.rem(e + n_ep // 2, n_ep)

    def remote(src, dst, send, recv, ep, tp):
        return pltpu.make_async_remote_copy(
            src_ref=src,
            dst_ref=dst,
            send_sem=send,
            recv_sem=recv,
            device_id=(ep, tp),
            device_id_type=pl.DeviceIdType.MESH,
        )

    def peer(r):
        return lax.rem(e + r, n_ep)

    load_wi = pltpu.make_async_copy(w_in, wi, w_sem.at[0])
    load_wo = pltpu.make_async_copy(w_out, wo, w_sem.at[1])
    load_wi.start()
    load_wo.start()

    barrier = pltpu.get_barrier_semaphore()

    def greet(r, c):
        pl.semaphore_signal(
            barrier, inc=1, device_id=(peer(r), t), device_id_type=pl.DeviceIdType.MESH
        )
        return c

    lax.fori_loop(1, n_ep, greet, 0)
    for who in (sib, up, dn):
        pl.semaphore_signal(barrier, inc=1, device_id=(e, who), device_id_type=pl.DeviceIdType.MESH)

    copy_ids = lax.broadcasted_iota(jnp.int32, (n_ep, ntok), 0)
    hits = jnp.zeros((n_ep, ntok), F32)
    weights = jnp.zeros((n_ep, ntok), F32)
    for k in range(routes.shape[0]):
        same = routes[k : k + 1, :] == copy_ids
        hits = jnp.where(same, 1.0, hits)
        weights = jnp.where(same, probs[k : k + 1, :], weights)
    before = (
        lax.broadcasted_iota(jnp.int32, (ntok, ntok), 0)
        < lax.broadcasted_iota(jnp.int32, (ntok, ntok), 1)
    )
    before = jnp.where(before, 1.0, 0.0).astype(BF16)
    named[...] = hits
    rank[...] = dot(hits.astype(BF16), before, ROWS)
    share[...] = weights
    slots = lax.broadcasted_iota(jnp.int32, (cap, ntok), 0).astype(F32)

    def place(c):
        mine = (named[pl.ds(c, 1), :] > 0.5) & (rank[pl.ds(c, 1), :] == slots)
        return jnp.where(mine, 1.0, 0.0)

    def block(c):
        return pl.ds(pl.multiple_of(c * cap, cap), cap)

    def rows_x(c):
        hot = place(c).astype(BF16)
        onehot[block(c), :] = hot
        return dot(hot, tok[...], ROWS).astype(BF16)

    def rows_g(c):
        hot = place(c)
        scale = jnp.sum(hot * share[pl.ds(c, 1), :], axis=1, keepdims=True)
        return (dot(hot.astype(BF16), og[...], ROWS) * scale).astype(BF16)

    pl.semaphore_wait(barrier, n_ep - 1 + 3)

    def dispatch(which, rows_of, pack, buf):
        def one(r, c):
            j = peer(r)
            pack[j] = rows_of(j)
            remote(
                pack.at[j], buf.at[t, block(e)], a_send.at[which, j], a_recv.at[which, e], j, t
            ).start()
            return c

        lax.fori_loop(1, n_ep, one, 0)
        buf[t, block(e), :] = rows_of(e)

    dispatch(0, rows_x, pack_x, xs)
    dispatch(1, rows_g, pack_g, gs)

    def arrived(which, pack, buf):
        def one(r, c):
            j = peer(r)
            remote(
                pack.at[j], buf.at[t, block(j)], a_send.at[which, j], a_recv.at[which, j], j, t
            ).wait_recv()
            return c

        lax.fori_loop(1, n_ep, one, 0)

    def unit(which, slot, h, send, to):
        buf = (xs, gs)[which]
        ref = buf.at[slot, pl.ds(h * half, half)]
        return remote(ref, ref, send, g_recv.at[which, slot, h], e, to)

    def to_up(which, n, slot, h):
        return unit(which, slot, h, ring_send.at[which, 0, n], up)

    def to_dn(which, n, slot, h):
        return unit(which, slot, h, ring_send.at[which, 1, n], dn)

    def to_sib(which, n, slot, h):
        return unit(which, slot, h, core_send.at[which, n, h], sib)

    def got(which, slot, h):
        unit(which, slot, h, core_send.at[which, 0, h], sib).wait_recv()

    def first_hop(which):
        to_up(which, 0, t, 0).start()
        to_dn(which, 0, t, 1).start()
        to_sib(which, 0, t, 0).start()
        to_sib(which, 0, t, 1).start()
        to_up(which, 1, t, 1).start()
        to_dn(which, 1, t, 0).start()

    def near(which, use):
        use(t)
        got(which, dn, 0)
        to_up(which, 2, dn, 0).start()
        to_sib(which, 1, dn, 0).start()
        got(which, up, 1)
        to_dn(which, 2, up, 1).start()
        to_sib(which, 2, up, 1).start()
        got(which, dn, 1)
        to_sib(which, 1, dn, 1).start()
        use(dn)
        got(which, up, 0)
        to_sib(which, 2, up, 0).start()
        use(up)

    def rest(which, use):
        for slot in (sib, sdn, sup):
            got(which, slot, 0)
            got(which, slot, 1)
            use(slot)
        got(which, far, 0)
        to_sib(which, 3, far, 0).start()
        got(which, far, 1)
        to_sib(which, 3, far, 1).start()
        use(far)
        got(which, sfar, 0)
        got(which, sfar, 1)
        use(sfar)

    def sent(which):
        for n in range(3):
            to_up(which, n, t, 0).wait_send()
            to_dn(which, n, t, 0).wait_send()
        for n in range(4):
            for h in range(2):
                to_sib(which, n, t, h).wait_send()

    def columns(slot):
        return pl.ds(pl.multiple_of(slot * width, width), width)

    def use_x(slot):
        def one(i, c):
            r = pl.ds(pl.multiple_of(i * tile, tile), tile)
            ab[:, r] += dot(wi[:, columns(slot)], xs[slot, r, :], LAST)
            return c

        lax.fori_loop(0, rows // tile, one, 0)

    def send_out(slot):
        return remote(
            own_out.at[slot], rec_out.at[slot], eo_send.at[slot], eo_recv.at[slot], other, t
        )

    def send_in(slot):
        return remote(own_in.at[slot], rec_in.at[slot], ei_send.at[slot], ei_recv.at[slot], other, t)

    def use_g(slot):
        def wgrad(i, c):
            w = pl.ds(pl.multiple_of(i * wide, wide), wide)
            own_out[slot, :, w] = dot(hid[...], gs[slot, :, w], ROWS).astype(BF16)
            return c

        lax.fori_loop(0, width // wide, wgrad, 0)
        send_out(slot).start()

        def one(i, c):
            r = pl.ds(pl.multiple_of(i * tile, tile), tile)
            dh[:, r] += dot(wo[:, columns(slot)], gs[slot, r, :], LAST)
            return c

        lax.fori_loop(0, rows // tile, one, 0)

    ab[...] = jnp.zeros_like(ab)
    dh[...] = jnp.zeros_like(dh)
    load_wi.wait()
    load_wo.wait()
    arrived(0, pack_x, xs)
    first_hop(0)
    near(0, use_x)
    arrived(1, pack_g, gs)
    first_hop(1)
    rest(0, use_x)

    def act(i, c):
        r = pl.ds(pl.multiple_of(i * lane, lane), lane)
        a, b = ab[0:ff, r], ab[ff : 2 * ff, r]
        hid[:, r] = (a * jax.nn.sigmoid(a) * b).astype(BF16)
        return c

    lax.fori_loop(0, rows // lane, act, 0)
    near(1, use_g)
    rest(1, use_g)

    def act_grad(i, c):
        r = pl.ds(pl.multiple_of(i * lane, lane), lane)
        a, b, d = ab[0:ff, r], ab[ff : 2 * ff, r], dh[:, r]
        s = jax.nn.sigmoid(a)
        da = d * b * s * (1.0 + a * (1.0 - s))
        db = d * (a * s)
        dadb_t[0:ff, r] = da.astype(BF16)
        dadb_t[ff : 2 * ff, r] = db.astype(BF16)
        dadb[r, :] = jnp.concatenate([da, db], axis=0).T.astype(BF16)
        return c

    lax.fori_loop(0, rows // lane, act_grad, 0)

    def wgrad_in(slot):
        def one(i, c):
            w = pl.ds(pl.multiple_of(i * wide, wide), wide)
            own_in[slot, :, w] = dot(dadb_t[...], xs[slot, :, w], ROWS).astype(BF16)
            return c

        lax.fori_loop(0, width // wide, one, 0)
        send_in(slot).start()

    def term(slot, dst, at):
        def one(i, c):
            r = pl.ds(pl.multiple_of(i * tile, tile), tile)
            dst[at, r, :] = dot(dadb[r, :], wi[:, columns(slot)], ROWS).astype(BF16)
            return c

        lax.fori_loop(0, rows // tile, one, 0)

    def send_part(at):
        return remote(part_sib.at[at], part_rec.at[at], p_send.at[at], p_recv.at[at], e, sib)

    for i, (yd, slot) in enumerate(((y_far, sfar), (y_up, sup), (y_dn, sdn), (y, sib))):
        wgrad_in(i)
        term(slot, part_sib, yd)
        send_part(yd).start()
    for i, (yd, slot) in enumerate(((y_far, far), (y_up, up), (y_dn, dn), (y, t))):
        wgrad_in(4 + i)
        term(slot, part, yd)

    def add(ref, at, src, src_at, h):
        r = pl.ds(h * half, half)
        ref[at, r, :] = (ref[at, r, :].astype(F32) + src[src_at, r, :].astype(F32)).astype(BF16)

    def chip(at):
        send_part(at).wait_recv()
        for h in range(2):
            add(part, at, part_rec, at, h)

    lower, upper = pl.ds(0, half), pl.ds(half, half)
    far_dn = remote(
        part.at[y_far, lower], half_rec.at[0, lower], h_send.at[0], h_recv.at[0], e, dn
    )
    far_up = remote(
        part.at[y_far, upper], half_rec.at[0, upper], h_send.at[1], h_recv.at[1], e, up
    )

    def full(direction, h):
        r = (lower, upper)[h]
        at, to = ((y_dn, dn), (y_up, up))[direction]
        return remote(
            part.at[at, r],
            full_rec.at[direction, r],
            f_send.at[direction, h],
            f_recv.at[direction, h],
            e,
            to,
        )

    chip(y_far)
    far_dn.start()
    far_up.start()
    chip(y_dn)
    full(0, 1).start()
    chip(y_up)
    full(1, 0).start()
    far_dn.wait_recv()
    add(part, y_dn, half_rec, 0, 0)
    full(0, 0).start()
    far_up.wait_recv()
    add(part, y_up, half_rec, 0, 1)
    full(1, 1).start()
    send_part(y).wait_recv()

    for h in range(2):
        full(0, h).wait_recv()
        full(1, h).wait_recv()

    def total(i, c):
        r = block(i)
        mine = part[y, r, :].astype(F32) + part_rec[y, r, :].astype(F32)
        ring = full_rec[0, r, :].astype(F32) + full_rec[1, r, :].astype(F32)
        part[y, r, :] = (mine + ring).astype(BF16)
        return c

    lax.fori_loop(0, n_ep, total, 0)

    def home(j, at):
        return remote(part.at[y, block(j)], back.at[block(at)], b_send.at[j], b_recv.at[at], j, t)

    def send_home(r, c):
        home(peer(r), e).start()
        return c

    lax.fori_loop(1, n_ep, send_home, 0)
    back[block(e), :] = part[y, block(e), :]

    def got_home(r, c):
        home(peer(r), peer(r)).wait_recv()
        return c

    lax.fori_loop(1, n_ep, got_home, 0)
    in_grad[...] = dot(onehot[...], back[...], FIRST).astype(BF16)

    def store_out(slot):
        return pltpu.make_async_copy(
            rec_out.at[slot], grad_out.at[:, columns(slot)], o_sem.at[0, slot]
        )

    def store_in(slot):
        return pltpu.make_async_copy(rec_in.at[slot], grad_in.at[:, columns(slot)], o_sem.at[1, slot])

    for slot in (t, dn, up, sib, sdn, sup, far, sfar):
        send_out(slot).wait_recv()
        rec_out[slot] = (rec_out[slot].astype(F32) + own_out[slot].astype(F32)).astype(BF16)
        store_out(slot).start()

    def merge(slot, c):
        send_in(slot).wait_recv()
        rec_in[slot] = (rec_in[slot].astype(F32) + own_in[slot].astype(F32)).astype(BF16)
        store_in(slot).start()
        return c

    lax.fori_loop(0, 2 * n_y, merge, 0)

    def end_peers(r, c):
        j = peer(r)
        for which, pack in ((0, pack_x), (1, pack_g)):
            remote(
                pack.at[j], pack.at[j], a_send.at[which, j], a_recv.at[which, j], j, t
            ).wait_send()
        home(j, e).wait_send()
        return c

    lax.fori_loop(1, n_ep, end_peers, 0)
    sent(0)
    sent(1)
    far_dn.wait_send()
    far_up.wait_send()
    for direction in range(2):
        for h in range(2):
            full(direction, h).wait_send()

    def end_parts(at, c):
        send_part(at).wait_send()
        return c

    lax.fori_loop(0, n_y, end_parts, 0)

    def end_grads(slot, c):
        send_out(slot).wait_send()
        send_in(slot).wait_send()
        store_out(slot).wait()
        store_in(slot).wait()
        return c

    lax.fori_loop(0, 2 * n_y, end_grads, 0)


def body(tokens, out_grad, routes, probs, w_in, w_out):
    n_ep = lax.axis_size("ep")
    n_tp = lax.axis_size("tp")
    n_y = n_tp // 2
    ntok, top = routes.shape
    cap = 2 * ntok * top // n_ep
    rows = n_ep * cap
    width = tokens.shape[1]
    ff = w_out.shape[1]
    depth = w_out.shape[2]
    half = rows // 2
    dma = pltpu.SemaphoreType.DMA
    vmem = pl.BlockSpec(memory_space=pltpu.VMEM)
    anywhere = pl.BlockSpec(memory_space=pl.ANY)
    flops = 2 * rows * depth * ff * 8
    in_grad, grad_in, grad_out = pl.pallas_call(
        functools.partial(kernel, n_ep, n_y),
        out_shape=(
            jax.ShapeDtypeStruct((ntok, width), BF16),
            jax.ShapeDtypeStruct((2 * ff, depth), BF16),
            jax.ShapeDtypeStruct((ff, depth), BF16),
        ),
        in_specs=[vmem, vmem, vmem, vmem, anywhere, anywhere],
        out_specs=(vmem, anywhere, anywhere),
        scratch_shapes=[
            pltpu.VMEM((n_tp, rows, width), BF16),
            pltpu.VMEM((n_tp, rows, width), BF16),
            pltpu.VMEM((2 * ff, depth), BF16),
            pltpu.VMEM((ff, depth), BF16),
            pltpu.VMEM((n_ep, cap, width), BF16),
            pltpu.VMEM((n_ep, cap, width), BF16),
            pltpu.VMEM((rows, ntok), BF16),
            pltpu.VMEM((n_ep, ntok), F32),
            pltpu.VMEM((n_ep, ntok), F32),
            pltpu.VMEM((n_ep, ntok), F32),
            pltpu.VMEM((2 * ff, rows), F32),
            pltpu.VMEM((ff, rows), F32),
            pltpu.VMEM((ff, rows), BF16),
            pltpu.VMEM((2 * ff, rows), BF16),
            pltpu.VMEM((rows, 2 * ff), BF16),
            pltpu.VMEM((n_tp, ff, width), BF16),
            pltpu.VMEM((n_tp, ff, width), BF16),
            pltpu.VMEM((n_tp, 2 * ff, width), BF16),
            pltpu.VMEM((n_tp, 2 * ff, width), BF16),
            pltpu.VMEM((n_y, rows, width), BF16),
            pltpu.VMEM((n_y, rows, width), BF16),
            pltpu.VMEM((n_y, rows, width), BF16),
            pltpu.VMEM((1, rows, width), BF16),
            pltpu.VMEM((2, rows, width), BF16),
            pltpu.VMEM((rows, width), BF16),
            dma((2,)),
            dma((2, n_ep)),
            dma((2, n_ep)),
            dma((2, 2, 3)),
            dma((2, 4, 2)),
            dma((2, n_tp, 2)),
            dma((n_tp,)),
            dma((n_tp,)),
            dma((n_tp,)),
            dma((n_tp,)),
            dma((n_y,)),
            dma((n_y,)),
            dma((2,)),
            dma((2,)),
            dma((2, 2)),
            dma((2, 2)),
            dma((n_ep,)),
            dma((n_ep,)),
            dma((2, n_tp)),
        ],
        compiler_params=pltpu.CompilerParams(
            collective_id=0, has_side_effects=True, vmem_limit_bytes=60 * 1024 * 1024
        ),
        cost_estimate=pl.CostEstimate(
            flops=flops, bytes_accessed=4 * rows * depth, transcendentals=2 * rows * ff
        ),
    )(
        tokens,
        out_grad,
        routes.T,
        probs.astype(F32).T,
        w_in.reshape(2 * ff, depth),
        w_out.reshape(ff, depth),
    )
    return in_grad, grad_in.reshape(1, 2, ff, depth), grad_out.reshape(1, ff, depth)


def solution(mesh):
    return jax.shard_map(
        body,
        mesh=mesh,
        in_specs=(
            P("ep", "tp"),
            P("ep", "tp"),
            P("ep", None),
            P("ep", None),
            P("ep", None, "tp", None),
            P("ep", "tp", None),
        ),
        out_specs=(P("ep", "tp"), P("ep", None, "tp", None), P("ep", "tp", None)),
        check_vma=False,
    )
```

```python
import functools

import jax
import jax.numpy as jnp
from jax import lax
from jax.experimental import pallas as pl
from jax.experimental.pallas import tpu as pltpu
from jax.sharding import PartitionSpec as P

BF16 = jnp.bfloat16
F32 = jnp.float32
LAST = (((1,), (1,)), ((), ()))
FIRST = (((0,), (0,)), ((), ()))
ROWS = (((1,), (0,)), ((), ()))


def dot(a, b, dims):
    return lax.dot_general(a, b, dims, preferred_element_type=F32)


def store(in_grad, grad_in, grad_out, in_grad_hbm, grad_in_hbm, grad_out_hbm, sems):
    copies = [
        pltpu.make_async_copy(src, dst, sems.at[i])
        for i, (src, dst) in enumerate(
            ((grad_in, grad_in_hbm), (grad_out, grad_out_hbm), (in_grad, in_grad_hbm))
        )
    ]
    for copy in copies:
        copy.start()
    for copy in copies:
        copy.wait()


def kernel(
    n_ep,
    n_y,
    tok_hbm,
    og_hbm,
    routes,
    probs,
    w_in,
    w_out,
    in_grad,
    grad_in,
    grad_out,
    tok,
    og,
    xs,
    gs,
    wi,
    wo,
    pack_x,
    pack_g,
    onehot,
    named,
    rank,
    share,
    ab,
    dh,
    hid,
    dadb_t,
    dadb,
    own_out,
    own_in,
    part_sib,
    part_rec,
    part,
    half_rec,
    full_rec,
    back,
    load_sem,
    a_send,
    a_recv,
    ring_send,
    core_send,
    g_recv,
    eo_send,
    eo_recv,
    ei_send,
    ei_recv,
    p_send,
    p_recv,
    h_send,
    h_recv,
    f_send,
    f_recv,
    b_send,
    b_recv,
):
    n_unit, rows, uw = xs.shape
    cap = rows // n_ep
    half = rows // 2
    width = tok.shape[1]
    ntok = tok.shape[0]
    ff = wo.shape[0]
    tile = min(256, rows)
    lane = min(128, rows)
    e = lax.axis_index("ep")
    t = lax.axis_index("tp")
    y = t // 2
    core = t % 2
    sib = y * 2 + (1 - core)
    y_up = lax.rem(y + 1, n_y)
    y_far = lax.rem(y + 2, n_y)
    y_dn = lax.rem(y + n_y - 1, n_y)
    up, far, dn = (v * 2 + core for v in (y_up, y_far, y_dn))
    sup, sfar, sdn = (v * 2 + (1 - core) for v in (y_up, y_far, y_dn))
    other = lax.rem(e + n_ep // 2, n_ep)

    def remote(src, dst, send, recv, ep, tp):
        return pltpu.make_async_remote_copy(
            src_ref=src,
            dst_ref=dst,
            send_sem=send,
            recv_sem=recv,
            device_id=(ep, tp),
            device_id_type=pl.DeviceIdType.MESH,
        )

    def peer(r):
        return lax.rem(e + r, n_ep)

    def signal(ep, tp):
        pl.semaphore_signal(
            barrier, inc=1, device_id=(ep, tp), device_id_type=pl.DeviceIdType.MESH
        )

    barrier = pltpu.get_barrier_semaphore()

    def greet(r, c):
        signal(peer(r), t)
        return c

    lax.fori_loop(1, n_ep, greet, 0)
    for who in (sib, up, dn):
        signal(e, who)

    load_tok, load_og, load_wi, load_wo = (
        pltpu.make_async_copy(src, dst, load_sem.at[i])
        for i, (src, dst) in enumerate(((tok_hbm, tok), (og_hbm, og), (w_in, wi), (w_out, wo)))
    )
    load_tok.start()
    load_og.start()
    load_wi.start()
    load_wo.start()

    copy_ids = lax.broadcasted_iota(jnp.int32, (n_ep, ntok), 0)
    hits = jnp.zeros((n_ep, ntok), F32)
    weights = jnp.zeros((n_ep, ntok), F32)
    shares = probs[...].astype(F32)
    for k in range(routes.shape[0]):
        same = routes[k : k + 1, :] == copy_ids
        hits = jnp.where(same, 1.0, hits)
        weights = jnp.where(same, shares[k : k + 1, :], weights)
    before = (
        lax.broadcasted_iota(jnp.int32, (ntok, ntok), 0)
        < lax.broadcasted_iota(jnp.int32, (ntok, ntok), 1)
    )
    before = jnp.where(before, 1.0, 0.0).astype(BF16)
    named[...] = hits
    rank[...] = dot(hits.astype(BF16), before, ROWS)
    share[...] = weights
    slots = lax.broadcasted_iota(jnp.int32, (cap, ntok), 0).astype(F32)

    def place(c):
        mine = (named[pl.ds(c, 1), :] > 0.5) & (rank[pl.ds(c, 1), :] == slots)
        return jnp.where(mine, 1.0, 0.0)

    def block(c):
        return pl.ds(pl.multiple_of(c * cap, cap), cap)

    def rows_x(c):
        hot = place(c).astype(BF16)
        onehot[block(c), :] = hot
        return dot(hot, tok[...], ROWS).astype(BF16)

    def rows_g(c):
        hot = place(c)
        scale = jnp.sum(hot * share[pl.ds(c, 1), :], axis=1, keepdims=True)
        return (dot(hot.astype(BF16), og[...], ROWS) * scale).astype(BF16)

    def pack_rows(rows_of, pack, buf):
        def one(r, c):
            j = peer(r)
            made = rows_of(j)
            for h in range(2):
                pack[j, h] = made[:, h * uw : (h + 1) * uw]
            return c

        lax.fori_loop(1, n_ep, one, 0)
        made = rows_of(e)
        for h in range(2):
            buf[t * 2 + h, block(e), :] = made[:, h * uw : (h + 1) * uw]

    packs, bufs = (pack_x, pack_g), (xs, gs)

    def rows_copy(which, h, j, at):
        return remote(
            packs[which].at[j, h],
            bufs[which].at[t * 2 + h, block(at)],
            a_send.at[which, h, j],
            a_recv.at[which, h, at],
            j,
            t,
        )

    def dispatch(which):
        for h in range(2):

            def one(r, c, h=h):
                rows_copy(which, h, peer(r), e).start()
                return c

            lax.fori_loop(1, n_ep, one, 0)

    def arrived(which, h):
        def one(r, c):
            rows_copy(which, h, peer(r), peer(r)).wait_recv()
            return c

        lax.fori_loop(1, n_ep, one, 0)

    load_tok.wait()
    pack_rows(rows_x, pack_x, xs)
    ab[...] = jnp.zeros_like(ab)
    dh[...] = jnp.zeros_like(dh)
    pl.semaphore_wait(barrier, n_ep - 1 + 3)
    dispatch(0)
    load_og.wait()
    pack_rows(rows_g, pack_g, gs)
    dispatch(1)
    load_wi.wait()
    load_wo.wait()

    def unit(which, slot, h, send, to):
        ref = bufs[which].at[slot * 2 + h]
        return remote(ref, ref, send, g_recv.at[which, slot * 2 + h], e, to)

    def to_up(which, n, slot, h):
        return unit(which, slot, h, ring_send.at[which, 0, n], up)

    def to_dn(which, n, slot, h):
        return unit(which, slot, h, ring_send.at[which, 1, n], dn)

    def to_sib(which, n, slot, h):
        return unit(which, slot, h, core_send.at[which, n, h], sib)

    def got(which, slot, h):
        unit(which, slot, h, core_send.at[which, 0, h], sib).wait_recv()

    def first_hop(which):
        for h in range(2):
            arrived(which, h)
            to_up(which, h, t, h).start()
            to_dn(which, h, t, h).start()
            to_sib(which, 0, t, h).start()

    def gather(which, use, between):
        use(t, 0)
        use(t, 1)
        for h in range(2):
            got(which, sib, h)
            use(sib, h)
        got(which, dn, 0)
        to_up(which, 2, dn, 0).start()
        to_sib(which, 1, dn, 0).start()
        got(which, up, 0)
        to_sib(which, 2, up, 0).start()
        use(dn, 0)
        use(up, 0)
        for slot in (sdn, sup):
            got(which, slot, 0)
            use(slot, 0)
        got(which, up, 1)
        to_dn(which, 2, up, 1).start()
        to_sib(which, 2, up, 1).start()
        got(which, dn, 1)
        to_sib(which, 1, dn, 1).start()
        between()
        use(dn, 1)
        use(up, 1)
        for slot in (sdn, sup):
            got(which, slot, 1)
            use(slot, 1)
        for h in range(2):
            got(which, far, h)
            to_sib(which, 3, far, h).start()
            use(far, h)
        for h in range(2):
            got(which, sfar, h)
            use(sfar, h)

    def sent(which):
        for n in range(3):
            to_up(which, n, t, 0).wait_send()
            to_dn(which, n, t, 0).wait_send()
        for n in range(4):
            for h in range(2):
                to_sib(which, n, t, h).wait_send()

    def columns(slot):
        return pl.ds(pl.multiple_of(slot * width, width), width)

    def ucolumns(u):
        return pl.ds(pl.multiple_of(u * uw, uw), uw)

    def use_x(slot, h):
        u = slot * 2 + h

        def one(i, c):
            r = pl.ds(pl.multiple_of(i * tile, tile), tile)
            ab[:, r] += dot(wi[:, ucolumns(u)], xs[u, r, :], LAST)
            return c

        lax.fori_loop(0, rows // tile, one, 0)

    def send_out(u):
        return remote(
            own_out.at[u], grad_out.at[:, ucolumns(u)], eo_send.at[u], eo_recv.at[u], other, t
        )

    def send_in(u):
        return remote(
            own_in.at[u], grad_in.at[:, ucolumns(u)], ei_send.at[u], ei_recv.at[u], other, t
        )

    def use_g(slot, h):
        u = slot * 2 + h
        own_out[u] = dot(hid[...], gs[u], ROWS).astype(BF16)
        send_out(u).start()

        def one(i, c):
            r = pl.ds(pl.multiple_of(i * tile, tile), tile)
            dh[:, r] += dot(wo[:, ucolumns(u)], gs[u, r, :], LAST)
            return c

        lax.fori_loop(0, rows // tile, one, 0)

    first_hop(0)
    gather(0, use_x, functools.partial(first_hop, 1))

    def act(i, c):
        r = pl.ds(pl.multiple_of(i * lane, lane), lane)
        a, b = ab[0:ff, r], ab[ff : 2 * ff, r]
        hid[:, r] = (a * jax.nn.sigmoid(a) * b).astype(BF16)
        return c

    lax.fori_loop(0, rows // lane, act, 0)
    gather(1, use_g, lambda: None)

    def act_grad(i, c):
        r = pl.ds(pl.multiple_of(i * lane, lane), lane)
        a, b, d = ab[0:ff, r], ab[ff : 2 * ff, r], dh[:, r]
        s = jax.nn.sigmoid(a)
        da = d * b * s * (1.0 + a * (1.0 - s))
        db = d * (a * s)
        dadb_t[0:ff, r] = da.astype(BF16)
        dadb_t[ff : 2 * ff, r] = db.astype(BF16)
        dadb[r, :] = jnp.concatenate([da, db], axis=0).T.astype(BF16)
        return c

    lax.fori_loop(0, rows // lane, act_grad, 0)

    def wgrad_in(u):
        own_in[u] = dot(dadb_t[...], xs[u], ROWS).astype(BF16)
        send_in(u).start()

    def term(slot, dst, at):
        def one(i, c):
            r = pl.ds(pl.multiple_of(i * tile, tile), tile)
            dst[at, r, :] = dot(dadb[r, :], wi[:, columns(slot)], ROWS).astype(BF16)
            return c

        lax.fori_loop(0, rows // tile, one, 0)

    def send_part(at):
        return remote(part_sib.at[at], part_rec.at[at], p_send.at[at], p_recv.at[at], e, sib)

    for i, (yd, slot) in enumerate(((y_far, sfar), (y_up, sup), (y_dn, sdn), (y, sib))):
        wgrad_in(2 * i)
        wgrad_in(2 * i + 1)
        term(slot, part_sib, yd)
        send_part(yd).start()
    for i, (yd, slot) in enumerate(((y_far, far), (y_up, up), (y_dn, dn), (y, t))):
        wgrad_in(8 + 2 * i)
        wgrad_in(9 + 2 * i)
        term(slot, part, yd)

    def add(ref, at, src, src_at, h):
        r = pl.ds(h * half, half)
        ref[at, r, :] = (ref[at, r, :].astype(F32) + src[src_at, r, :].astype(F32)).astype(BF16)

    def chip(at):
        send_part(at).wait_recv()
        for h in range(2):
            add(part, at, part_rec, at, h)

    lower, upper = pl.ds(0, half), pl.ds(half, half)
    far_dn = remote(
        part.at[y_far, lower], half_rec.at[0, lower], h_send.at[0], h_recv.at[0], e, dn
    )
    far_up = remote(
        part.at[y_far, upper], half_rec.at[0, upper], h_send.at[1], h_recv.at[1], e, up
    )

    def full(direction, h):
        r = (lower, upper)[h]
        at, to = ((y_dn, dn), (y_up, up))[direction]
        return remote(
            part.at[at, r],
            full_rec.at[direction, r],
            f_send.at[direction, h],
            f_recv.at[direction, h],
            e,
            to,
        )

    chip(y_far)
    far_dn.start()
    far_up.start()
    chip(y_dn)
    full(0, 1).start()
    chip(y_up)
    full(1, 0).start()
    far_dn.wait_recv()
    add(part, y_dn, half_rec, 0, 0)
    full(0, 0).start()
    far_up.wait_recv()
    add(part, y_up, half_rec, 0, 1)
    full(1, 1).start()
    send_part(y).wait_recv()

    for h in range(2):
        full(0, h).wait_recv()
        full(1, h).wait_recv()

    def total(i, c):
        r = block(i)
        mine = part[y, r, :].astype(F32) + part_rec[y, r, :].astype(F32)
        ring = full_rec[0, r, :].astype(F32) + full_rec[1, r, :].astype(F32)
        part[y, r, :] = (mine + ring).astype(BF16)
        return c

    lax.fori_loop(0, n_ep, total, 0)

    def home(j, at):
        return remote(part.at[y, block(j)], back.at[block(at)], b_send.at[j], b_recv.at[at], j, t)

    def send_home(r, c):
        home(peer(r), e).start()
        return c

    lax.fori_loop(1, n_ep, send_home, 0)
    back[block(e), :] = part[y, block(e), :]

    def merge_out(u, c):
        send_out(u).wait_recv()
        w = ucolumns(u)
        grad_out[:, w] = (grad_out[:, w].astype(F32) + own_out[u].astype(F32)).astype(BF16)
        return c

    lax.fori_loop(0, n_unit, merge_out, 0)

    def got_home(r, c):
        home(peer(r), peer(r)).wait_recv()
        return c

    lax.fori_loop(1, n_ep, got_home, 0)
    in_grad[...] = dot(onehot[...], back[...], FIRST).astype(BF16)

    def merge_in(u, c):
        send_in(u).wait_recv()
        w = ucolumns(u)
        grad_in[:, w] = (grad_in[:, w].astype(F32) + own_in[u].astype(F32)).astype(BF16)
        return c

    lax.fori_loop(0, n_unit, merge_in, 0)

    def end_peers(r, c):
        j = peer(r)
        for which in range(2):
            for h in range(2):
                rows_copy(which, h, j, e).wait_send()
        home(j, e).wait_send()
        return c

    lax.fori_loop(1, n_ep, end_peers, 0)
    sent(0)
    sent(1)
    far_dn.wait_send()
    far_up.wait_send()
    for direction in range(2):
        for h in range(2):
            full(direction, h).wait_send()

    def end_parts(at, c):
        send_part(at).wait_send()
        return c

    lax.fori_loop(0, n_y, end_parts, 0)

    def end_grads(u, c):
        send_out(u).wait_send()
        send_in(u).wait_send()
        return c

    lax.fori_loop(0, n_unit, end_grads, 0)


def body(tokens, out_grad, routes, probs, w_in, w_out):
    n_ep = lax.axis_size("ep")
    n_tp = lax.axis_size("tp")
    n_y = n_tp // 2
    n_unit = 2 * n_tp
    ntok, top = routes.shape
    cap = 2 * ntok * top // n_ep
    rows = n_ep * cap
    width = tokens.shape[1]
    uw = width // 2
    ff = w_out.shape[1]
    depth = w_out.shape[2]
    dma = pltpu.SemaphoreType.DMA
    vmem = pl.BlockSpec(memory_space=pltpu.VMEM)
    anywhere = pl.BlockSpec(memory_space=pl.ANY)
    flops = 2 * rows * depth * ff * 8
    made = pl.pallas_call(
        functools.partial(kernel, n_ep, n_y),
        out_shape=(
            pltpu.VMEM((ntok, width), BF16),
            pltpu.VMEM((2 * ff, depth), BF16),
            pltpu.VMEM((ff, depth), BF16),
        ),
        in_specs=[anywhere, anywhere, vmem, vmem, anywhere, anywhere],
        out_specs=(vmem, vmem, vmem),
        scratch_shapes=[
            pltpu.VMEM((ntok, width), BF16),
            pltpu.VMEM((ntok, width), BF16),
            pltpu.VMEM((n_unit, rows, uw), BF16),
            pltpu.VMEM((n_unit, rows, uw), BF16),
            pltpu.VMEM((2 * ff, depth), BF16),
            pltpu.VMEM((ff, depth), BF16),
            pltpu.VMEM((n_ep, 2, cap, uw), BF16),
            pltpu.VMEM((n_ep, 2, cap, uw), BF16),
            pltpu.VMEM((rows, ntok), BF16),
            pltpu.VMEM((n_ep, ntok), F32),
            pltpu.VMEM((n_ep, ntok), F32),
            pltpu.VMEM((n_ep, ntok), F32),
            pltpu.VMEM((2 * ff, rows), F32),
            pltpu.VMEM((ff, rows), F32),
            pltpu.VMEM((ff, rows), BF16),
            pltpu.VMEM((2 * ff, rows), BF16),
            pltpu.VMEM((rows, 2 * ff), BF16),
            pltpu.VMEM((n_unit, ff, uw), BF16),
            pltpu.VMEM((n_unit, 2 * ff, uw), BF16),
            pltpu.VMEM((n_y, rows, width), BF16),
            pltpu.VMEM((n_y, rows, width), BF16),
            pltpu.VMEM((n_y, rows, width), BF16),
            pltpu.VMEM((1, rows, width), BF16),
            pltpu.VMEM((2, rows, width), BF16),
            pltpu.VMEM((rows, width), BF16),
            dma((4,)),
            dma((2, 2, n_ep)),
            dma((2, 2, n_ep)),
            dma((2, 2, 3)),
            dma((2, 4, 2)),
            dma((2, n_unit)),
            dma((n_unit,)),
            dma((n_unit,)),
            dma((n_unit,)),
            dma((n_unit,)),
            dma((n_y,)),
            dma((n_y,)),
            dma((2,)),
            dma((2,)),
            dma((2, 2)),
            dma((2, 2)),
            dma((n_ep,)),
            dma((n_ep,)),
        ],
        compiler_params=pltpu.CompilerParams(
            collective_id=0, has_side_effects=True, vmem_limit_bytes=56 * 1024 * 1024
        ),
        cost_estimate=pl.CostEstimate(
            flops=flops, bytes_accessed=4 * rows * depth, transcendentals=2 * rows * ff
        ),
    )(
        tokens,
        out_grad,
        routes.T,
        probs.T,
        w_in.reshape(2 * ff, depth),
        w_out.reshape(ff, depth),
    )
    in_grad, grad_in, grad_out = pl.pallas_call(
        store,
        out_shape=tuple(jax.ShapeDtypeStruct(m.shape, BF16) for m in made),
        in_specs=[anywhere] * 3,
        out_specs=(anywhere,) * 3,
        scratch_shapes=[dma((3,))],
        compiler_params=pltpu.CompilerParams(vmem_limit_bytes=1024 * 1024),
    )(*(pltpu.with_memory_space_constraint(m, pltpu.VMEM) for m in made))
    return in_grad, grad_in.reshape(1, 2, ff, depth), grad_out.reshape(1, ff, depth)


def solution(mesh):
    return jax.shard_map(
        body,
        mesh=mesh,
        in_specs=(
            P("ep", "tp"),
            P("ep", "tp"),
            P("ep", None),
            P("ep", None),
            P("ep", None, "tp", None),
            P("ep", "tp", None),
        ),
        out_specs=(P("ep", "tp"), P("ep", None, "tp", None), P("ep", "tp", None)),
        check_vma=False,
    )
```

```python
import functools

import jax
import jax.numpy as jnp
from jax import lax
from jax.experimental import pallas as pl
from jax.experimental.pallas import tpu as pltpu
from jax.sharding import PartitionSpec as P

BF16 = jnp.bfloat16
F32 = jnp.float32
LAST = (((1,), (1,)), ((), ()))
FIRST = (((0,), (0,)), ((), ()))
ROWS = (((1,), (0,)), ((), ()))


def dot(a, b, dims):
    return lax.dot_general(a, b, dims, preferred_element_type=F32)


def store(in_grad, grad_in, grad_out, in_grad_hbm, grad_in_hbm, grad_out_hbm, sems):
    copies = [
        pltpu.make_async_copy(src, dst, sems.at[i])
        for i, (src, dst) in enumerate(
            ((grad_in, grad_in_hbm), (grad_out, grad_out_hbm), (in_grad, in_grad_hbm))
        )
    ]
    for copy in copies:
        copy.start()
    for copy in copies:
        copy.wait()


def kernel(
    n_ep,
    n_y,
    tok_hbm,
    og_hbm,
    routes,
    probs,
    w_in,
    w_out,
    in_grad,
    grad_in,
    grad_out,
    tok,
    tok_far,
    og,
    xs,
    gs,
    wi,
    wo,
    pack_x,
    pack_g,
    pack_far,
    onehot,
    named,
    rank,
    share,
    ab,
    dh,
    hid,
    dadb_t,
    dadb,
    own_out,
    own_in,
    part_sib,
    part_rec,
    part,
    half_rec,
    full_rec,
    back,
    load_sem,
    t_send,
    t_recv,
    a_send,
    a_recv,
    ring_send,
    core_send,
    g_recv,
    eo_send,
    eo_recv,
    ei_send,
    ei_recv,
    p_send,
    p_recv,
    h_send,
    h_recv,
    f_send,
    f_recv,
    b_send,
    b_recv,
):
    n_unit, rows, uw = xs.shape
    cap = rows // n_ep
    half = rows // 2
    width = tok.shape[1]
    ntok = tok.shape[0]
    ff = wo.shape[0]
    tile = min(256, rows)
    lane = min(128, rows)
    e = lax.axis_index("ep")
    t = lax.axis_index("tp")
    y = t // 2
    core = t % 2
    sib = y * 2 + (1 - core)
    y_up = lax.rem(y + 1, n_y)
    y_far = lax.rem(y + 2, n_y)
    y_dn = lax.rem(y + n_y - 1, n_y)
    up, far, dn = (v * 2 + core for v in (y_up, y_far, y_dn))
    sup, sfar, sdn = (v * 2 + (1 - core) for v in (y_up, y_far, y_dn))
    other = lax.rem(e + n_ep // 2, n_ep)

    def remote(src, dst, send, recv, ep, tp):
        return pltpu.make_async_remote_copy(
            src_ref=src,
            dst_ref=dst,
            send_sem=send,
            recv_sem=recv,
            device_id=(ep, tp),
            device_id_type=pl.DeviceIdType.MESH,
        )

    def peer(r):
        return lax.rem(e + r, n_ep)

    def signal(ep, tp):
        pl.semaphore_signal(
            barrier, inc=1, device_id=(ep, tp), device_id_type=pl.DeviceIdType.MESH
        )

    barrier = pltpu.get_barrier_semaphore()

    def greet(r, c):
        signal(peer(r), t)
        return c

    lax.fori_loop(1, n_ep, greet, 0)
    for who in (sib, up, dn, far):
        signal(e, who)

    load_tok, load_og, load_wi, load_wo = (
        pltpu.make_async_copy(src, dst, load_sem.at[i])
        for i, (src, dst) in enumerate(((tok_hbm, tok), (og_hbm, og), (w_in, wi), (w_out, wo)))
    )
    load_tok.start()
    load_og.start()
    load_wi.start()
    load_wo.start()

    copy_ids = lax.broadcasted_iota(jnp.int32, (n_ep, ntok), 0)
    hits = jnp.zeros((n_ep, ntok), F32)
    weights = jnp.zeros((n_ep, ntok), F32)
    shares = probs[...].astype(F32)
    for k in range(routes.shape[0]):
        same = routes[k : k + 1, :] == copy_ids
        hits = jnp.where(same, 1.0, hits)
        weights = jnp.where(same, shares[k : k + 1, :], weights)
    before = (
        lax.broadcasted_iota(jnp.int32, (ntok, ntok), 0)
        < lax.broadcasted_iota(jnp.int32, (ntok, ntok), 1)
    )
    before = jnp.where(before, 1.0, 0.0).astype(BF16)
    named[...] = hits
    rank[...] = dot(hits.astype(BF16), before, ROWS)
    share[...] = weights
    slots = lax.broadcasted_iota(jnp.int32, (cap, ntok), 0).astype(F32)

    def place(c):
        mine = (named[pl.ds(c, 1), :] > 0.5) & (rank[pl.ds(c, 1), :] == slots)
        return jnp.where(mine, 1.0, 0.0)

    def block(c):
        return pl.ds(pl.multiple_of(c * cap, cap), cap)

    def rows_x(c):
        hot = place(c).astype(BF16)
        onehot[block(c), :] = hot
        return dot(hot, tok[...], ROWS).astype(BF16)

    def rows_g(c):
        hot = place(c)
        scale = jnp.sum(hot * share[pl.ds(c, 1), :], axis=1, keepdims=True)
        return (dot(hot.astype(BF16), og[...], ROWS) * scale).astype(BF16)

    def rows_far(c):
        return dot(onehot[block(c), :], tok_far[...], ROWS).astype(BF16)

    def pack_rows(rows_of, pack, buf, slot):
        def one(r, c):
            j = peer(r)
            made = rows_of(j)
            for h in range(2):
                pack[j, h] = made[:, h * uw : (h + 1) * uw]
            return c

        lax.fori_loop(1, n_ep, one, 0)
        made = rows_of(e)
        for h in range(2):
            buf[slot * 2 + h, block(e), :] = made[:, h * uw : (h + 1) * uw]

    packs, bufs, own = (pack_x, pack_g, pack_far), (xs, gs, xs), (t, t, far)

    def rows_copy(which, h, j, at):
        return remote(
            packs[which].at[j, h],
            bufs[which].at[own[which] * 2 + h, block(at)],
            a_send.at[which, h, j],
            a_recv.at[which, h, at],
            j,
            t,
        )

    def dispatch(which, h):
        def one(r, c):
            rows_copy(which, h, peer(r), e).start()
            return c

        lax.fori_loop(1, n_ep, one, 0)

    def arrived(which, h):
        def one(r, c):
            rows_copy(which, h, peer(r), peer(r)).wait_recv()
            return c

        lax.fori_loop(1, n_ep, one, 0)

    load_tok.wait()
    pack_rows(rows_x, pack_x, xs, t)
    ab[...] = jnp.zeros_like(ab)
    dh[...] = jnp.zeros_like(dh)
    pl.semaphore_wait(barrier, n_ep - 1 + 4)
    tokens_far = remote(tok, tok_far, t_send.at[0], t_recv.at[0], e, far)
    tokens_far.start()
    dispatch(0, 0)
    dispatch(0, 1)
    load_og.wait()
    pack_rows(rows_g, pack_g, gs, t)
    tokens_far.wait_recv()
    pack_rows(rows_far, pack_far, xs, far)
    load_wi.wait()
    load_wo.wait()

    def unit(which, slot, h, send, to):
        ref = bufs[which].at[slot * 2 + h]
        return remote(ref, ref, send, g_recv.at[which, slot * 2 + h], e, to)

    def to_up(which, n, slot, h):
        return unit(which, slot, h, ring_send.at[which, 0, n], up)

    def to_dn(which, n, slot, h):
        return unit(which, slot, h, ring_send.at[which, 1, n], dn)

    def to_sib(which, n, slot, h):
        return unit(which, slot, h, core_send.at[which, n, h], sib)

    def got(which, slot, h):
        unit(which, slot, h, core_send.at[which, 0, h], sib).wait_recv()

    def first_hop(which, h):
        arrived(which, h)
        to_up(which, h, t, h).start()
        to_dn(which, h, t, h).start()
        to_sib(which, 0, t, h).start()

    def gather_x(use):
        use(t, 0)
        use(t, 1)
        for h in range(2):
            got(0, sib, h)
            use(sib, h)
        for h in range(2):
            got(0, dn, h)
            to_sib(0, 1, dn, h).start()
            got(0, up, h)
            to_sib(0, 2, up, h).start()
            if h == 1:
                first_hop(1, 0)
            use(dn, h)
            use(up, h)
            arrived(2, h)
            to_sib(0, 3, far, h).start()
            use(far, h)
            for slot in (sdn, sup, sfar):
                got(0, slot, h)
                use(slot, h)

    def gather_g(use):
        use(t, 0)
        use(t, 1)
        for h in range(2):
            got(1, sib, h)
            use(sib, h)
        got(1, dn, 0)
        to_up(1, 2, dn, 0).start()
        to_sib(1, 1, dn, 0).start()
        got(1, up, 0)
        to_sib(1, 2, up, 0).start()
        use(dn, 0)
        use(up, 0)
        for slot in (sdn, sup):
            got(1, slot, 0)
            use(slot, 0)
        got(1, up, 1)
        to_dn(1, 2, up, 1).start()
        to_sib(1, 2, up, 1).start()
        got(1, dn, 1)
        to_sib(1, 1, dn, 1).start()
        use(dn, 1)
        use(up, 1)
        for slot in (sdn, sup):
            got(1, slot, 1)
            use(slot, 1)
        for h in range(2):
            got(1, far, h)
            to_sib(1, 3, far, h).start()
            use(far, h)
        for h in range(2):
            got(1, sfar, h)
            use(sfar, h)

    def sent(which):
        for n in range(2 + which):
            to_up(which, n, t, 0).wait_send()
            to_dn(which, n, t, 0).wait_send()
        for n in range(4):
            for h in range(2):
                to_sib(which, n, t, h).wait_send()

    def columns(slot):
        return pl.ds(pl.multiple_of(slot * width, width), width)

    def ucolumns(u):
        return pl.ds(pl.multiple_of(u * uw, uw), uw)

    def use_x(slot, h):
        u = slot * 2 + h

        def one(i, c):
            r = pl.ds(pl.multiple_of(i * tile, tile), tile)
            ab[:, r] += dot(wi[:, ucolumns(u)], xs[u, r, :], LAST)
            return c

        lax.fori_loop(0, rows // tile, one, 0)

    def send_out(u):
        return remote(
            own_out.at[u], grad_out.at[:, ucolumns(u)], eo_send.at[u], eo_recv.at[u], other, t
        )

    def send_in(u):
        return remote(
            own_in.at[u], grad_in.at[:, ucolumns(u)], ei_send.at[u], ei_recv.at[u], other, t
        )

    def use_g(slot, h):
        u = slot * 2 + h
        own_out[u] = dot(hid[...], gs[u], ROWS).astype(BF16)
        send_out(u).start()

        def one(i, c):
            r = pl.ds(pl.multiple_of(i * tile, tile), tile)
            dh[:, r] += dot(wo[:, ucolumns(u)], gs[u, r, :], LAST)
            return c

        lax.fori_loop(0, rows // tile, one, 0)

    first_hop(0, 0)
    dispatch(2, 0)
    dispatch(2, 1)
    first_hop(0, 1)
    dispatch(1, 0)
    dispatch(1, 1)
    gather_x(use_x)
    first_hop(1, 1)

    def act(i, c):
        r = pl.ds(pl.multiple_of(i * lane, lane), lane)
        a, b = ab[0:ff, r], ab[ff : 2 * ff, r]
        hid[:, r] = (a * jax.nn.sigmoid(a) * b).astype(BF16)
        return c

    lax.fori_loop(0, rows // lane, act, 0)
    gather_g(use_g)

    def act_grad(i, c):
        r = pl.ds(pl.multiple_of(i * lane, lane), lane)
        a, b, d = ab[0:ff, r], ab[ff : 2 * ff, r], dh[:, r]
        s = jax.nn.sigmoid(a)
        da = d * b * s * (1.0 + a * (1.0 - s))
        db = d * (a * s)
        dadb_t[0:ff, r] = da.astype(BF16)
        dadb_t[ff : 2 * ff, r] = db.astype(BF16)
        dadb[r, :] = jnp.concatenate([da, db], axis=0).T.astype(BF16)
        return c

    lax.fori_loop(0, rows // lane, act_grad, 0)

    def wgrad_in(u):
        own_in[u] = dot(dadb_t[...], xs[u], ROWS).astype(BF16)
        send_in(u).start()

    def term(slot, dst, at):
        def one(i, c):
            r = pl.ds(pl.multiple_of(i * tile, tile), tile)
            dst[at, r, :] = dot(dadb[r, :], wi[:, columns(slot)], ROWS).astype(BF16)
            return c

        lax.fori_loop(0, rows // tile, one, 0)

    def send_part(at):
        return remote(part_sib.at[at], part_rec.at[at], p_send.at[at], p_recv.at[at], e, sib)

    for i, (yd, slot) in enumerate(((y_far, sfar), (y_up, sup), (y_dn, sdn), (y, sib))):
        wgrad_in(2 * i)
        wgrad_in(2 * i + 1)
        term(slot, part_sib, yd)
        send_part(yd).start()
    for i, (yd, slot) in enumerate(((y_far, far), (y_up, up), (y_dn, dn), (y, t))):
        wgrad_in(8 + 2 * i)
        wgrad_in(9 + 2 * i)
        term(slot, part, yd)

    def add(ref, at, src, src_at, h):
        r = pl.ds(h * half, half)
        ref[at, r, :] = (ref[at, r, :].astype(F32) + src[src_at, r, :].astype(F32)).astype(BF16)

    def chip(at):
        send_part(at).wait_recv()
        for h in range(2):
            add(part, at, part_rec, at, h)

    lower, upper = pl.ds(0, half), pl.ds(half, half)
    far_dn = remote(
        part.at[y_far, lower], half_rec.at[0, lower], h_send.at[0], h_recv.at[0], e, dn
    )
    far_up = remote(
        part.at[y_far, upper], half_rec.at[0, upper], h_send.at[1], h_recv.at[1], e, up
    )

    def full(direction, h):
        r = (lower, upper)[h]
        at, to = ((y_dn, dn), (y_up, up))[direction]
        return remote(
            part.at[at, r],
            full_rec.at[direction, r],
            f_send.at[direction, h],
            f_recv.at[direction, h],
            e,
            to,
        )

    chip(y_far)
    far_dn.start()
    far_up.start()
    chip(y_dn)
    full(0, 1).start()
    chip(y_up)
    full(1, 0).start()
    far_dn.wait_recv()
    add(part, y_dn, half_rec, 0, 0)
    full(0, 0).start()
    far_up.wait_recv()
    add(part, y_up, half_rec, 0, 1)
    full(1, 1).start()
    send_part(y).wait_recv()

    for h in range(2):
        full(0, h).wait_recv()
        full(1, h).wait_recv()

    def total(i, c):
        r = block(i)
        mine = part[y, r, :].astype(F32) + part_rec[y, r, :].astype(F32)
        ring = full_rec[0, r, :].astype(F32) + full_rec[1, r, :].astype(F32)
        part[y, r, :] = (mine + ring).astype(BF16)
        return c

    lax.fori_loop(0, n_ep, total, 0)

    def home(j, at):
        return remote(part.at[y, block(j)], back.at[block(at)], b_send.at[j], b_recv.at[at], j, t)

    def send_home(r, c):
        home(peer(r), e).start()
        return c

    lax.fori_loop(1, n_ep, send_home, 0)
    back[block(e), :] = part[y, block(e), :]

    def merge_out(u, c):
        send_out(u).wait_recv()
        w = ucolumns(u)
        grad_out[:, w] = (grad_out[:, w].astype(F32) + own_out[u].astype(F32)).astype(BF16)
        return c

    lax.fori_loop(0, n_unit, merge_out, 0)

    def got_home(r, c):
        home(peer(r), peer(r)).wait_recv()
        return c

    lax.fori_loop(1, n_ep, got_home, 0)
    in_grad[...] = dot(onehot[...], back[...], FIRST).astype(BF16)

    def merge_in(u, c):
        send_in(u).wait_recv()
        w = ucolumns(u)
        grad_in[:, w] = (grad_in[:, w].astype(F32) + own_in[u].astype(F32)).astype(BF16)
        return c

    lax.fori_loop(0, n_unit, merge_in, 0)

    def end_peers(r, c):
        j = peer(r)
        for which in range(3):
            for h in range(2):
                rows_copy(which, h, j, e).wait_send()
        home(j, e).wait_send()
        return c

    lax.fori_loop(1, n_ep, end_peers, 0)
    sent(0)
    sent(1)
    tokens_far.wait_send()
    far_dn.wait_send()
    far_up.wait_send()
    for direction in range(2):
        for h in range(2):
            full(direction, h).wait_send()

    def end_parts(at, c):
        send_part(at).wait_send()
        return c

    lax.fori_loop(0, n_y, end_parts, 0)

    def end_grads(u, c):
        send_out(u).wait_send()
        send_in(u).wait_send()
        return c

    lax.fori_loop(0, n_unit, end_grads, 0)


def body(tokens, out_grad, routes, probs, w_in, w_out):
    n_ep = lax.axis_size("ep")
    n_tp = lax.axis_size("tp")
    n_y = n_tp // 2
    n_unit = 2 * n_tp
    ntok, top = routes.shape
    cap = 2 * ntok * top // n_ep
    rows = n_ep * cap
    width = tokens.shape[1]
    uw = width // 2
    ff = w_out.shape[1]
    depth = w_out.shape[2]
    dma = pltpu.SemaphoreType.DMA
    vmem = pl.BlockSpec(memory_space=pltpu.VMEM)
    anywhere = pl.BlockSpec(memory_space=pl.ANY)
    flops = 2 * rows * depth * ff * 8
    made = pl.pallas_call(
        functools.partial(kernel, n_ep, n_y),
        out_shape=(
            pltpu.VMEM((ntok, width), BF16),
            pltpu.VMEM((2 * ff, depth), BF16),
            pltpu.VMEM((ff, depth), BF16),
        ),
        in_specs=[anywhere, anywhere, vmem, vmem, anywhere, anywhere],
        out_specs=(vmem, vmem, vmem),
        scratch_shapes=[
            pltpu.VMEM((ntok, width), BF16),
            pltpu.VMEM((ntok, width), BF16),
            pltpu.VMEM((ntok, width), BF16),
            pltpu.VMEM((n_unit, rows, uw), BF16),
            pltpu.VMEM((n_unit, rows, uw), BF16),
            pltpu.VMEM((2 * ff, depth), BF16),
            pltpu.VMEM((ff, depth), BF16),
            pltpu.VMEM((n_ep, 2, cap, uw), BF16),
            pltpu.VMEM((n_ep, 2, cap, uw), BF16),
            pltpu.VMEM((n_ep, 2, cap, uw), BF16),
            pltpu.VMEM((rows, ntok), BF16),
            pltpu.VMEM((n_ep, ntok), F32),
            pltpu.VMEM((n_ep, ntok), F32),
            pltpu.VMEM((n_ep, ntok), F32),
            pltpu.VMEM((2 * ff, rows), F32),
            pltpu.VMEM((ff, rows), F32),
            pltpu.VMEM((ff, rows), BF16),
            pltpu.VMEM((2 * ff, rows), BF16),
            pltpu.VMEM((rows, 2 * ff), BF16),
            pltpu.VMEM((n_unit, ff, uw), BF16),
            pltpu.VMEM((n_unit, 2 * ff, uw), BF16),
            pltpu.VMEM((n_y, rows, width), BF16),
            pltpu.VMEM((n_y, rows, width), BF16),
            pltpu.VMEM((n_y, rows, width), BF16),
            pltpu.VMEM((1, rows, width), BF16),
            pltpu.VMEM((2, rows, width), BF16),
            pltpu.VMEM((rows, width), BF16),
            dma((4,)),
            dma((1,)),
            dma((1,)),
            dma((3, 2, n_ep)),
            dma((3, 2, n_ep)),
            dma((2, 2, 3)),
            dma((2, 4, 2)),
            dma((2, n_unit)),
            dma((n_unit,)),
            dma((n_unit,)),
            dma((n_unit,)),
            dma((n_unit,)),
            dma((n_y,)),
            dma((n_y,)),
            dma((2,)),
            dma((2,)),
            dma((2, 2)),
            dma((2, 2)),
            dma((n_ep,)),
            dma((n_ep,)),
        ],
        compiler_params=pltpu.CompilerParams(
            collective_id=0, has_side_effects=True, vmem_limit_bytes=56 * 1024 * 1024
        ),
        cost_estimate=pl.CostEstimate(
            flops=flops, bytes_accessed=4 * rows * depth, transcendentals=2 * rows * ff
        ),
    )(
        tokens,
        out_grad,
        routes.T,
        probs.T,
        w_in.reshape(2 * ff, depth),
        w_out.reshape(ff, depth),
    )
    in_grad, grad_in, grad_out = pl.pallas_call(
        store,
        out_shape=tuple(jax.ShapeDtypeStruct(m.shape, BF16) for m in made),
        in_specs=[anywhere] * 3,
        out_specs=(anywhere,) * 3,
        scratch_shapes=[dma((3,))],
        compiler_params=pltpu.CompilerParams(vmem_limit_bytes=1024 * 1024),
    )(*(pltpu.with_memory_space_constraint(m, pltpu.VMEM) for m in made))
    return in_grad, grad_in.reshape(1, 2, ff, depth), grad_out.reshape(1, ff, depth)


def solution(mesh):
    return jax.shard_map(
        body,
        mesh=mesh,
        in_specs=(
            P("ep", "tp"),
            P("ep", "tp"),
            P("ep", None),
            P("ep", None),
            P("ep", None, "tp", None),
            P("ep", "tp", None),
        ),
        out_specs=(P("ep", "tp"), P("ep", None, "tp", None), P("ep", "tp", None)),
        check_vma=False,
    )
```

```python
import functools
import math

import jax
import jax.numpy as jnp
from jax import lax
from jax.experimental import pallas as pl
from jax.experimental.pallas import tpu as pltpu
from jax.sharding import PartitionSpec as P

BF16 = jnp.bfloat16
F32 = jnp.float32
LAST = (((1,), (1,)), ((), ()))
FIRST = (((0,), (0,)), ((), ()))
ROWS = (((1,), (0,)), ((), ()))


def dot(a, b, dims):
    return lax.dot_general(a, b, dims, preferred_element_type=F32)


def store(in_grad, grad_in, grad_out, in_grad_hbm, grad_in_hbm, grad_out_hbm, sems):
    copies = [
        pltpu.make_async_copy(src, dst, sems.at[i])
        for i, (src, dst) in enumerate(
            ((grad_in, grad_in_hbm), (grad_out, grad_out_hbm), (in_grad, in_grad_hbm))
        )
    ]
    for copy in copies:
        copy.start()
    for copy in copies:
        copy.wait()


def kernel(
    n_ep,
    n_y,
    tok_hbm,
    og_hbm,
    routes,
    probs,
    w_in,
    w_out,
    in_grad,
    grad_in,
    grad_out,
    tok,
    tok_far,
    og,
    xs,
    gs,
    wi,
    wo,
    pack_x,
    pack_g,
    pack_far,
    onehot,
    codes,
    share,
    ab,
    dh,
    hid,
    dadb_t,
    dadb,
    own_out,
    own_in,
    part_sib,
    part_rec,
    part,
    half_rec,
    full_rec,
    back,
    token_sum,
    token_rec,
    load_sem,
    t_send,
    t_recv,
    a_send,
    a_recv,
    ring_send,
    core_send,
    g_recv,
    fr_send,
    fr_recv,
    fc_send,
    fc_recv,
    eo_send,
    eo_recv,
    ei_send,
    ei_recv,
    p_send,
    p_recv,
    h_send,
    h_recv,
    f_send,
    f_recv,
    z_send,
    z_recv,
    c_send,
    c_recv,
):
    n_unit, rows, uw = xs.shape
    cap = rows // n_ep
    half = rows // 2
    uq = uw // 2
    width = tok.shape[1]
    ntok = tok.shape[0]
    ff = wo.shape[0]
    tile = min(256, rows)
    lane = min(128, rows)
    e = lax.axis_index("ep")
    t = lax.axis_index("tp")
    y = t // 2
    core = t % 2
    sib = y * 2 + (1 - core)
    y_up = lax.rem(y + 1, n_y)
    y_far = lax.rem(y + 2, n_y)
    y_dn = lax.rem(y + n_y - 1, n_y)
    up, far, dn = (v * 2 + core for v in (y_up, y_far, y_dn))
    sup, sfar, sdn = (v * 2 + (1 - core) for v in (y_up, y_far, y_dn))
    n_z = math.isqrt(n_ep)
    n_x = n_ep // n_z
    x = e // n_z
    z = e % n_z
    other = lax.rem(e + n_ep // 2, n_ep)

    def remote(src, dst, send, recv, ep, tp):
        return pltpu.make_async_remote_copy(
            src_ref=src,
            dst_ref=dst,
            send_sem=send,
            recv_sem=recv,
            device_id=(ep, tp),
            device_id_type=pl.DeviceIdType.MESH,
        )

    def peer(r):
        return lax.rem(e + r, n_ep)

    def signal(ep, tp):
        pl.semaphore_signal(
            barrier, inc=1, device_id=(ep, tp), device_id_type=pl.DeviceIdType.MESH
        )

    barrier = pltpu.get_barrier_semaphore()

    def greet(r, c):
        signal(peer(r), t)
        return c

    lax.fori_loop(1, n_ep, greet, 0)
    for who in (sib, up, dn, far):
        signal(e, who)

    load_tok, load_og, load_wi, load_wo = (
        pltpu.make_async_copy(src, dst, load_sem.at[i])
        for i, (src, dst) in enumerate(((tok_hbm, tok), (og_hbm, og), (w_in, wi), (w_out, wo)))
    )
    load_tok.start()
    load_og.start()
    load_wi.start()
    load_wo.start()

    copy_ids = lax.broadcasted_iota(jnp.int32, (n_ep, ntok), 0)
    hits = jnp.zeros((n_ep, ntok), F32)
    weights = jnp.zeros((n_ep, ntok), F32)
    shares = probs[...].astype(F32)
    for k in range(routes.shape[0]):
        same = routes[k : k + 1, :] == copy_ids
        hits = jnp.where(same, 1.0, hits)
        weights = jnp.where(same, shares[k : k + 1, :], weights)
    before = (
        lax.broadcasted_iota(jnp.int32, (ntok, ntok), 0)
        < lax.broadcasted_iota(jnp.int32, (ntok, ntok), 1)
    )
    before = jnp.where(before, 1.0, 0.0).astype(BF16)
    codes[x] = jnp.where(hits > 0.5, dot(hits.astype(BF16), before, ROWS), -1.0)
    share[...] = weights
    slots = lax.broadcasted_iota(jnp.int32, (cap, ntok), 0).astype(F32)

    def place(block_x, c):
        return jnp.where(codes[block_x, pl.ds(c, 1), :] == slots, 1.0, 0.0)

    def block(c):
        return pl.ds(pl.multiple_of(c * cap, cap), cap)

    def pack_rows(source, pack, buf, slot, scaled):
        group = min(4, n_ep)
        for g in range(0, n_ep, group):
            made = dot(onehot[g * cap : (g + group) * cap, :], source[...], ROWS)
            for k in range(group):
                c = g + k
                rows_c = made[k * cap : (k + 1) * cap]
                if scaled:
                    hot = onehot[c * cap : (c + 1) * cap, :].astype(F32)
                    rows_c = rows_c * jnp.sum(hot * share[c : c + 1, :], axis=1, keepdims=True)
                for h in range(2):
                    pack[c, h] = rows_c[:, h * uw : (h + 1) * uw].astype(BF16)
        for h in range(2):
            buf[slot * 2 + h, block(e), :] = pack[e, h]

    packs, bufs, own = (pack_x, pack_g, pack_far), (xs, gs, xs), (t, t, far)

    def rows_copy(which, h, j, at):
        return remote(
            packs[which].at[j, h],
            bufs[which].at[own[which] * 2 + h, block(at)],
            a_send.at[which, h, j],
            a_recv.at[which, h, at],
            j,
            t,
        )

    def dispatch(which, h):
        def one(r, c):
            rows_copy(which, h, peer(r), e).start()
            return c

        lax.fori_loop(1, n_ep, one, 0)

    def arrived(which, h):
        def one(r, c):
            rows_copy(which, h, peer(r), peer(r)).wait_recv()
            return c

        lax.fori_loop(1, n_ep, one, 0)

    for c in range(n_ep):
        onehot[c * cap : (c + 1) * cap, :] = place(x, c).astype(BF16)
    load_tok.wait()
    pack_rows(tok, pack_x, xs, t, False)
    pl.semaphore_wait(barrier, n_ep - 1 + 4)
    tokens_far = remote(tok, tok_far, t_send.at[0], t_recv.at[0], e, far)
    tokens_far.start()
    dispatch(0, 0)
    dispatch(0, 1)

    def code_copy(r, at):
        to = lax.rem(x + r, n_x)
        return remote(
            codes.at[x], codes.at[at], c_send.at[0, r], c_recv.at[0, at], to * n_z + z, t
        )

    def send_code(r, c):
        code_copy(r, x).start()
        return c

    lax.fori_loop(1, n_x, send_code, 0)
    ab[...] = jnp.zeros_like(ab)
    dh[...] = jnp.zeros_like(dh)
    tokens_far.wait_recv()
    pack_rows(tok_far, pack_far, xs, far, False)

    def unit(which, slot, h, send, to):
        ref = bufs[which].at[slot * 2 + h]
        return remote(ref, ref, send, g_recv.at[which, slot * 2 + h], e, to)

    def to_up(which, n, slot, h):
        return unit(which, slot, h, ring_send.at[which, 0, n], up)

    def to_dn(which, n, slot, h):
        return unit(which, slot, h, ring_send.at[which, 1, n], dn)

    def to_sib(which, n, slot, h):
        return unit(which, slot, h, core_send.at[which, n, h], sib)

    def got(which, slot, h):
        unit(which, slot, h, core_send.at[which, 0, h], sib).wait_recv()

    def first_hop(which, h):
        arrived(which, h)
        to_up(which, h, t, h).start()
        to_dn(which, h, t, h).start()
        to_sib(which, 0, t, h).start()

    def gather_x(use):
        use(t, 0)
        use(t, 1)
        for h in range(2):
            got(0, sib, h)
            use(sib, h)
        for h in range(2):
            got(0, dn, h)
            to_sib(0, 1, dn, h).start()
            got(0, up, h)
            to_sib(0, 2, up, h).start()
            if h == 1:
                first_hop(1, 0)
            use(dn, h)
            use(up, h)
            arrived(2, h)
            to_sib(0, 3, far, h).start()
            use(far, h)
            for slot in (sdn, sup, sfar):
                got(0, slot, h)
                use(slot, h)

    def quarter(slot, h, q, send, recv, to):
        ref = gs.at[slot * 2 + h, :, q * uq : (q + 1) * uq]
        return remote(ref, ref, send, recv, e, to)

    def far_ring(slot, h, q):
        return quarter(slot, h, q, fr_send.at[h, q], fr_recv.at[h, q], (up, dn)[h])

    def far_core(slot, h, q):
        return quarter(slot, h, q, fc_send.at[h, q], fc_recv.at[h, q], sib)

    def gather_g(use, use_far):
        use(t, 0)
        use(t, 1)
        for h in range(2):
            got(1, sib, h)
            use(sib, h)
        got(1, dn, 0)
        for q in range(2):
            far_ring(dn, 0, q).start()
        to_sib(1, 1, dn, 0).start()
        got(1, up, 0)
        to_sib(1, 2, up, 0).start()
        use(dn, 0)
        use(up, 0)
        for slot in (sdn, sup):
            got(1, slot, 0)
            use(slot, 0)
        got(1, up, 1)
        for q in range(2):
            far_ring(up, 1, q).start()
        to_sib(1, 2, up, 1).start()
        got(1, dn, 1)
        to_sib(1, 1, dn, 1).start()
        use(dn, 1)
        use(up, 1)
        for slot in (sdn, sup):
            got(1, slot, 1)
            use(slot, 1)
        for q in range(2):
            for h in range(2):
                far_ring(far, h, q).wait_recv()
                far_core(far, h, q).start()
                use_far(far, h, q)
            for h in range(2):
                far_core(sfar, h, q).wait_recv()
                use_far(sfar, h, q)

    def sent(which):
        for n in range(2):
            to_up(which, n, t, 0).wait_send()
            to_dn(which, n, t, 0).wait_send()
        for n in range(4 - which):
            for h in range(2):
                to_sib(which, n, t, h).wait_send()

    def columns(slot):
        return pl.ds(pl.multiple_of(slot * width, width), width)

    def ucolumns(u):
        return pl.ds(pl.multiple_of(u * uw, uw), uw)

    def use_x(slot, h):
        u = slot * 2 + h

        def one(i, c):
            r = pl.ds(pl.multiple_of(i * tile, tile), tile)
            ab[:, r] += dot(wi[:, ucolumns(u)], xs[u, r, :], LAST)
            return c

        lax.fori_loop(0, rows // tile, one, 0)

    def send_out(u, q):
        w = pl.ds(pl.multiple_of(u * uw + q * uq, uq), uq)
        return remote(
            own_out.at[u, :, q * uq : (q + 1) * uq],
            grad_out.at[:, w],
            eo_send.at[u, q],
            eo_recv.at[u, q],
            other,
            t,
        )

    def send_in(u):
        return remote(
            own_in.at[u], grad_in.at[:, ucolumns(u)], ei_send.at[u], ei_recv.at[u], other, t
        )

    def use_g(slot, h):
        u = slot * 2 + h
        own_out[u] = dot(hid[...], gs[u], ROWS).astype(BF16)
        for q in range(2):
            send_out(u, q).start()

        def one(i, c):
            r = pl.ds(pl.multiple_of(i * tile, tile), tile)
            dh[:, r] += dot(wo[:, ucolumns(u)], gs[u, r, :], LAST)
            return c

        lax.fori_loop(0, rows // tile, one, 0)

    def use_g_far(slot, h, q):
        u = slot * 2 + h
        w = slice(q * uq, (q + 1) * uq)
        own_out[u, :, w] = dot(hid[...], gs[u, :, w], ROWS).astype(BF16)
        send_out(u, q).start()
        cols = pl.ds(pl.multiple_of(u * uw + q * uq, uq), uq)

        def one(i, c):
            r = pl.ds(pl.multiple_of(i * tile, tile), tile)
            dh[:, r] += dot(wo[:, cols], gs[u, r, w], LAST)
            return c

        lax.fori_loop(0, rows // tile, one, 0)

    first_hop(0, 0)
    dispatch(2, 0)
    dispatch(2, 1)
    first_hop(0, 1)
    load_og.wait()
    pack_rows(og, pack_g, gs, t, True)
    load_wi.wait()
    load_wo.wait()
    dispatch(1, 0)
    dispatch(1, 1)
    gather_x(use_x)
    first_hop(1, 1)

    def act(i, c):
        r = pl.ds(pl.multiple_of(i * lane, lane), lane)
        a, b = ab[0:ff, r], ab[ff : 2 * ff, r]
        hid[:, r] = (a * jax.nn.sigmoid(a) * b).astype(BF16)
        return c

    lax.fori_loop(0, rows // lane, act, 0)
    gather_g(use_g, use_g_far)

    def act_grad(i, c):
        r = pl.ds(pl.multiple_of(i * lane, lane), lane)
        a, b, d = ab[0:ff, r], ab[ff : 2 * ff, r], dh[:, r]
        s = jax.nn.sigmoid(a)
        da = d * b * s * (1.0 + a * (1.0 - s))
        db = d * (a * s)
        dadb_t[0:ff, r] = da.astype(BF16)
        dadb_t[ff : 2 * ff, r] = db.astype(BF16)
        dadb[r, :] = jnp.concatenate([da, db], axis=0).T.astype(BF16)
        return c

    lax.fori_loop(0, rows // lane, act_grad, 0)

    def wgrad_in(u):
        own_in[u] = dot(dadb_t[...], xs[u], ROWS).astype(BF16)
        send_in(u).start()

    def term(slot, dst, at):
        def one(i, c):
            r = pl.ds(pl.multiple_of(i * tile, tile), tile)
            dst[at, r, :] = dot(dadb[r, :], wi[:, columns(slot)], ROWS).astype(BF16)
            return c

        lax.fori_loop(0, rows // tile, one, 0)

    def send_part(at):
        return remote(part_sib.at[at], part_rec.at[at], p_send.at[at], p_recv.at[at], e, sib)

    for i, (yd, slot) in enumerate(((y_far, sfar), (y_up, sup), (y_dn, sdn), (y, sib))):
        wgrad_in(2 * i)
        wgrad_in(2 * i + 1)
        term(slot, part_sib, yd)
        send_part(yd).start()
    for i, (yd, slot) in enumerate(((y_far, far), (y_up, up), (y_dn, dn), (y, t))):
        wgrad_in(8 + 2 * i)
        wgrad_in(9 + 2 * i)
        term(slot, part, yd)

    def add(ref, at, src, src_at, h):
        r = pl.ds(h * half, half)
        ref[at, r, :] = (ref[at, r, :].astype(F32) + src[src_at, r, :].astype(F32)).astype(BF16)

    def chip(at):
        send_part(at).wait_recv()
        for h in range(2):
            add(part, at, part_rec, at, h)

    lower, upper = pl.ds(0, half), pl.ds(half, half)
    far_dn = remote(
        part.at[y_far, lower], half_rec.at[0, lower], h_send.at[0], h_recv.at[0], e, dn
    )
    far_up = remote(
        part.at[y_far, upper], half_rec.at[0, upper], h_send.at[1], h_recv.at[1], e, up
    )

    def full(direction, h):
        r = (lower, upper)[h]
        at, to = ((y_dn, dn), (y_up, up))[direction]
        return remote(
            part.at[at, r],
            full_rec.at[direction, r],
            f_send.at[direction, h],
            f_recv.at[direction, h],
            e,
            to,
        )

    chip(y_far)
    far_dn.start()
    far_up.start()
    chip(y_dn)
    full(0, 1).start()
    chip(y_up)
    full(1, 0).start()
    far_dn.wait_recv()
    add(part, y_dn, half_rec, 0, 0)
    full(0, 0).start()
    far_up.wait_recv()
    add(part, y_up, half_rec, 0, 1)
    full(1, 1).start()
    send_part(y).wait_recv()

    for h in range(2):
        full(0, h).wait_recv()
        full(1, h).wait_recv()

    def total(i, c):
        r = block(i)
        mine = part[y, r, :].astype(F32) + part_rec[y, r, :].astype(F32)
        ring = full_rec[0, r, :].astype(F32) + full_rec[1, r, :].astype(F32)
        part[y, r, :] = (mine + ring).astype(BF16)
        return c

    lax.fori_loop(0, n_ep, total, 0)

    def along_z(r, at, bx):
        to = lax.rem(z + r, n_z)
        return remote(
            part.at[y, block(bx * n_z + to)],
            back.at[bx, at],
            z_send.at[r, bx],
            z_recv.at[at, bx],
            x * n_z + to,
            t,
        )

    def send_z(r, c):
        for bx in range(n_x):
            along_z(r, z, bx).start()
        return c

    lax.fori_loop(1, n_z, send_z, 0)
    for bx in range(n_x):
        back[bx, z] = part[y, block(bx * n_z + z), :]

    def merge_out(u, c):
        for q in range(2):
            send_out(u, q).wait_recv()
        w = ucolumns(u)
        grad_out[:, w] = (grad_out[:, w].astype(F32) + own_out[u].astype(F32)).astype(BF16)
        return c

    lax.fori_loop(0, n_unit, merge_out, 0)

    def got_code(r, c):
        code_copy(r, lax.rem(x + r, n_x)).wait_recv()
        return c

    lax.fori_loop(1, n_x, got_code, 0)

    def got_z(r, c):
        for bx in range(n_x):
            along_z(r, lax.rem(z + r, n_z), bx).wait_recv()
        return c

    lax.fori_loop(1, n_z, got_z, 0)

    def along_x(r, at):
        to = lax.rem(x + r, n_x)
        return remote(
            token_sum.at[to], token_rec.at[at], c_send.at[1, r], c_recv.at[1, at], to * n_z + z, t
        )

    def by_token(r, c):
        bx = lax.rem(x + r, n_x)
        hot = jnp.concatenate([place(bx, x * n_z + k) for k in range(n_z)], axis=0).astype(BF16)
        returned = jnp.concatenate([back[bx, k] for k in range(n_z)], axis=0)
        token_sum[bx] = dot(hot, returned, FIRST).astype(BF16)
        return c

    def send_x(r, c):
        by_token(r, c)
        along_x(r, x).start()
        return c

    lax.fori_loop(1, n_x, send_x, 0)
    by_token(0, 0)
    token_rec[x] = token_sum[x]

    def got_x(r, c):
        along_x(r, lax.rem(x + r, n_x)).wait_recv()
        return c

    lax.fori_loop(1, n_x, got_x, 0)
    in_grad[...] = jnp.sum(token_rec[...].astype(F32), axis=0).astype(BF16)

    def merge_in(u, c):
        send_in(u).wait_recv()
        w = ucolumns(u)
        grad_in[:, w] = (grad_in[:, w].astype(F32) + own_in[u].astype(F32)).astype(BF16)
        return c

    lax.fori_loop(0, n_unit, merge_in, 0)

    def end_peers(r, c):
        j = peer(r)
        for which in range(3):
            for h in range(2):
                rows_copy(which, h, j, e).wait_send()
        return c

    lax.fori_loop(1, n_ep, end_peers, 0)

    def end_z(r, c):
        for bx in range(n_x):
            along_z(r, z, bx).wait_send()
        return c

    lax.fori_loop(1, n_z, end_z, 0)

    def end_x(r, c):
        code_copy(r, x).wait_send()
        along_x(r, x).wait_send()
        return c

    lax.fori_loop(1, n_x, end_x, 0)
    sent(0)
    sent(1)
    tokens_far.wait_send()
    for h in range(2):
        for q in range(2):
            far_ring(far, h, q).wait_send()
            far_core(far, h, q).wait_send()
    far_dn.wait_send()
    far_up.wait_send()
    for direction in range(2):
        for h in range(2):
            full(direction, h).wait_send()

    def end_parts(at, c):
        send_part(at).wait_send()
        return c

    lax.fori_loop(0, n_y, end_parts, 0)

    def end_grads(u, c):
        for q in range(2):
            send_out(u, q).wait_send()
        send_in(u).wait_send()
        return c

    lax.fori_loop(0, n_unit, end_grads, 0)


def body(tokens, out_grad, routes, probs, w_in, w_out):
    n_ep = lax.axis_size("ep")
    n_tp = lax.axis_size("tp")
    n_y = n_tp // 2
    n_unit = 2 * n_tp
    n_z = math.isqrt(n_ep)
    n_x = n_ep // n_z
    ntok, top = routes.shape
    cap = 2 * ntok * top // n_ep
    rows = n_ep * cap
    width = tokens.shape[1]
    uw = width // 2
    ff = w_out.shape[1]
    depth = w_out.shape[2]
    dma = pltpu.SemaphoreType.DMA
    vmem = pl.BlockSpec(memory_space=pltpu.VMEM)
    anywhere = pl.BlockSpec(memory_space=pl.ANY)
    flops = 2 * rows * depth * ff * 8
    made = pl.pallas_call(
        functools.partial(kernel, n_ep, n_y),
        out_shape=(
            pltpu.VMEM((ntok, width), BF16),
            pltpu.VMEM((2 * ff, depth), BF16),
            pltpu.VMEM((ff, depth), BF16),
        ),
        in_specs=[anywhere, anywhere, vmem, vmem, anywhere, anywhere],
        out_specs=(vmem, vmem, vmem),
        scratch_shapes=[
            pltpu.VMEM((ntok, width), BF16),
            pltpu.VMEM((ntok, width), BF16),
            pltpu.VMEM((ntok, width), BF16),
            pltpu.VMEM((n_unit, rows, uw), BF16),
            pltpu.VMEM((n_unit, rows, uw), BF16),
            pltpu.VMEM((2 * ff, depth), BF16),
            pltpu.VMEM((ff, depth), BF16),
            pltpu.VMEM((n_ep, 2, cap, uw), BF16),
            pltpu.VMEM((n_ep, 2, cap, uw), BF16),
            pltpu.VMEM((n_ep, 2, cap, uw), BF16),
            pltpu.VMEM((rows, ntok), BF16),
            pltpu.VMEM((n_x, n_ep, ntok), F32),
            pltpu.VMEM((n_ep, ntok), F32),
            pltpu.VMEM((2 * ff, rows), F32),
            pltpu.VMEM((ff, rows), F32),
            pltpu.VMEM((ff, rows), BF16),
            pltpu.VMEM((2 * ff, rows), BF16),
            pltpu.VMEM((rows, 2 * ff), BF16),
            pltpu.VMEM((n_unit, ff, uw), BF16),
            pltpu.VMEM((n_unit, 2 * ff, uw), BF16),
            pltpu.VMEM((n_y, rows, width), BF16),
            pltpu.VMEM((n_y, rows, width), BF16),
            pltpu.VMEM((n_y, rows, width), BF16),
            pltpu.VMEM((1, rows, width), BF16),
            pltpu.VMEM((2, rows, width), BF16),
            pltpu.VMEM((n_x, n_z, cap, width), BF16),
            pltpu.VMEM((n_x, ntok, width), BF16),
            pltpu.VMEM((n_x, ntok, width), BF16),
            dma((4,)),
            dma((1,)),
            dma((1,)),
            dma((3, 2, n_ep)),
            dma((3, 2, n_ep)),
            dma((2, 2, 2)),
            dma((2, 4, 2)),
            dma((2, n_unit)),
            dma((2, 2)),
            dma((2, 2)),
            dma((2, 2)),
            dma((2, 2)),
            dma((n_unit, 2)),
            dma((n_unit, 2)),
            dma((n_unit,)),
            dma((n_unit,)),
            dma((n_y,)),
            dma((n_y,)),
            dma((2,)),
            dma((2,)),
            dma((2, 2)),
            dma((2, 2)),
            dma((n_z, n_x)),
            dma((n_z, n_x)),
            dma((2, n_x)),
            dma((2, n_x)),
        ],
        compiler_params=pltpu.CompilerParams(
            collective_id=0, has_side_effects=True, vmem_limit_bytes=56 * 1024 * 1024
        ),
        cost_estimate=pl.CostEstimate(
            flops=flops, bytes_accessed=4 * rows * depth, transcendentals=2 * rows * ff
        ),
    )(
        tokens,
        out_grad,
        routes.T,
        probs.T,
        w_in.reshape(2 * ff, depth),
        w_out.reshape(ff, depth),
    )
    in_grad, grad_in, grad_out = pl.pallas_call(
        store,
        out_shape=tuple(jax.ShapeDtypeStruct(m.shape, BF16) for m in made),
        in_specs=[anywhere] * 3,
        out_specs=(anywhere,) * 3,
        scratch_shapes=[dma((3,))],
        compiler_params=pltpu.CompilerParams(vmem_limit_bytes=1024 * 1024),
    )(*(pltpu.with_memory_space_constraint(m, pltpu.VMEM) for m in made))
    return in_grad, grad_in.reshape(1, 2, ff, depth), grad_out.reshape(1, ff, depth)


def solution(mesh):
    return jax.shard_map(
        body,
        mesh=mesh,
        in_specs=(
            P("ep", "tp"),
            P("ep", "tp"),
            P("ep", None),
            P("ep", None),
            P("ep", None, "tp", None),
            P("ep", "tp", None),
        ),
        out_specs=(P("ep", "tp"), P("ep", None, "tp", None), P("ep", "tp", None)),
        check_vma=False,
    )
```

```python
import functools
import math

import jax
import jax.numpy as jnp
from jax import lax
from jax.experimental import pallas as pl
from jax.experimental.pallas import tpu as pltpu
from jax.sharding import PartitionSpec as P

BF16 = jnp.bfloat16
F32 = jnp.float32
LAST = (((1,), (1,)), ((), ()))
FIRST = (((0,), (0,)), ((), ()))
ROWS = (((1,), (0,)), ((), ()))


def dot(a, b, dims):
    return lax.dot_general(a, b, dims, preferred_element_type=F32)


def store(in_grad, grad_in, grad_out, in_grad_hbm, grad_in_hbm, grad_out_hbm, sems):
    copies = [
        pltpu.make_async_copy(src, dst, sems.at[i])
        for i, (src, dst) in enumerate(
            ((grad_in, grad_in_hbm), (grad_out, grad_out_hbm), (in_grad, in_grad_hbm))
        )
    ]
    for copy in copies:
        copy.start()
    for copy in copies:
        copy.wait()


def kernel(
    n_ep,
    n_y,
    tok_hbm,
    og_hbm,
    routes,
    probs,
    w_in,
    w_out,
    in_grad,
    grad_in,
    grad_out,
    tok,
    tok_far,
    og,
    xs,
    gs,
    wi,
    wo,
    pack_x,
    pack_g,
    pack_far,
    onehot,
    codes,
    share,
    ab,
    dh,
    hid,
    dadb_t,
    dadb,
    own_out,
    own_in,
    part_sib,
    part_rec,
    part,
    half_rec,
    full_rec,
    back,
    token_sum,
    token_rec,
    load_sem,
    t_send,
    t_recv,
    a_send,
    a_recv,
    ring_send,
    core_send,
    g_recv,
    fr_send,
    fr_recv,
    fc_send,
    fc_recv,
    eo_send,
    eo_recv,
    ei_send,
    ei_recv,
    p_send,
    p_recv,
    h_send,
    h_recv,
    f_send,
    f_recv,
    z_send,
    z_recv,
    c_send,
    c_recv,
):
    n_unit, rows, uw = xs.shape
    cap = rows // n_ep
    half = rows // 2
    uq = uw // 2
    width = tok.shape[1]
    ntok = tok.shape[0]
    ff = wo.shape[0]
    tile = min(256, rows)
    lane = min(128, rows)
    e = lax.axis_index("ep")
    t = lax.axis_index("tp")
    y = t // 2
    core = t % 2
    sib = y * 2 + (1 - core)
    y_up = lax.rem(y + 1, n_y)
    y_far = lax.rem(y + 2, n_y)
    y_dn = lax.rem(y + n_y - 1, n_y)
    up, far, dn = (v * 2 + core for v in (y_up, y_far, y_dn))
    sup, sfar, sdn = (v * 2 + (1 - core) for v in (y_up, y_far, y_dn))
    n_z = math.isqrt(n_ep)
    n_x = n_ep // n_z
    x = e // n_z
    z = e % n_z
    other = lax.rem(e + n_ep // 2, n_ep)

    def remote(src, dst, send, recv, ep, tp):
        return pltpu.make_async_remote_copy(
            src_ref=src,
            dst_ref=dst,
            send_sem=send,
            recv_sem=recv,
            device_id=(ep, tp),
            device_id_type=pl.DeviceIdType.MESH,
        )

    def peer(r):
        return lax.rem(e + r, n_ep)

    def signal(ep, tp):
        pl.semaphore_signal(
            barrier, inc=1, device_id=(ep, tp), device_id_type=pl.DeviceIdType.MESH
        )

    barrier = pltpu.get_barrier_semaphore()

    def greet(r, c):
        signal(peer(r), t)
        return c

    lax.fori_loop(1, n_ep, greet, 0)
    for who in (sib, up, dn, far):
        signal(e, who)

    load_tok, load_og, load_wi, load_wo = (
        pltpu.make_async_copy(src, dst, load_sem.at[i])
        for i, (src, dst) in enumerate(((tok_hbm, tok), (og_hbm, og), (w_in, wi), (w_out, wo)))
    )
    load_tok.start()
    load_og.start()
    load_wi.start()
    load_wo.start()

    copy_ids = lax.broadcasted_iota(jnp.int32, (n_ep, ntok), 0)
    hits = jnp.zeros((n_ep, ntok), F32)
    weights = jnp.zeros((n_ep, ntok), F32)
    shares = probs[...].astype(F32)
    for k in range(routes.shape[0]):
        same = routes[k : k + 1, :] == copy_ids
        hits = jnp.where(same, 1.0, hits)
        weights = jnp.where(same, shares[k : k + 1, :], weights)
    before = (
        lax.broadcasted_iota(jnp.int32, (ntok, ntok), 0)
        < lax.broadcasted_iota(jnp.int32, (ntok, ntok), 1)
    )
    before = jnp.where(before, 1.0, 0.0).astype(BF16)
    codes[x] = jnp.where(hits > 0.5, dot(hits.astype(BF16), before, ROWS), -1.0)
    share[...] = weights
    slots = lax.broadcasted_iota(jnp.int32, (cap, ntok), 0).astype(F32)

    def place(block_x, c):
        return jnp.where(codes[block_x, pl.ds(c, 1), :] == slots, 1.0, 0.0)

    def block(c):
        return pl.ds(pl.multiple_of(c * cap, cap), cap)

    def weighted(c):
        return jnp.where(codes[x, pl.ds(c, 1), :] == slots, share[pl.ds(c, 1), :], 0.0)

    def pack_rows(source, pack, buf, slot, scaled):
        group = min(4, n_ep)
        for g in range(0, n_ep, group):
            hot = onehot[g * cap : (g + group) * cap, :]
            if scaled:
                hot = jnp.concatenate([weighted(g + k) for k in range(group)]).astype(BF16)
            made = dot(hot, source[...], ROWS).astype(BF16)
            for k in range(group):
                for h in range(2):
                    pack[g + k, h] = made[k * cap : (k + 1) * cap, h * uw : (h + 1) * uw]
        for h in range(2):
            buf[slot * 2 + h, block(e), :] = pack[e, h]

    packs, bufs, own = (pack_x, pack_g, pack_far), (xs, gs, xs), (t, t, far)

    def rows_copy(which, h, j, at):
        return remote(
            packs[which].at[j, h],
            bufs[which].at[own[which] * 2 + h, block(at)],
            a_send.at[which, h, j],
            a_recv.at[which, h, at],
            j,
            t,
        )

    def dispatch(which, h):
        def one(r, c):
            rows_copy(which, h, peer(r), e).start()
            return c

        lax.fori_loop(1, n_ep, one, 0)

    def arrived(which, h):
        def one(r, c):
            rows_copy(which, h, peer(r), peer(r)).wait_recv()
            return c

        lax.fori_loop(1, n_ep, one, 0)

    for c in range(n_ep):
        onehot[c * cap : (c + 1) * cap, :] = place(x, c).astype(BF16)
    load_tok.wait()
    pack_rows(tok, pack_x, xs, t, False)
    pl.semaphore_wait(barrier, n_ep - 1 + 4)
    tokens_far = remote(tok, tok_far, t_send.at[0], t_recv.at[0], e, far)
    tokens_far.start()
    dispatch(0, 0)
    dispatch(0, 1)

    def code_copy(r, at):
        to = lax.rem(x + r, n_x)
        return remote(
            codes.at[x], codes.at[at], c_send.at[0, r], c_recv.at[0, at], to * n_z + z, t
        )

    def send_code(r, c):
        code_copy(r, x).start()
        return c

    lax.fori_loop(1, n_x, send_code, 0)
    ab[...] = jnp.zeros_like(ab)
    dh[...] = jnp.zeros_like(dh)
    tokens_far.wait_recv()
    pack_rows(tok_far, pack_far, xs, far, False)

    def unit(which, slot, h, send, to):
        ref = bufs[which].at[slot * 2 + h]
        return remote(ref, ref, send, g_recv.at[which, slot * 2 + h], e, to)

    def to_up(which, n, slot, h):
        return unit(which, slot, h, ring_send.at[which, 0, n], up)

    def to_dn(which, n, slot, h):
        return unit(which, slot, h, ring_send.at[which, 1, n], dn)

    def to_sib(which, n, slot, h):
        return unit(which, slot, h, core_send.at[which, n, h], sib)

    def got(which, slot, h):
        unit(which, slot, h, core_send.at[which, 0, h], sib).wait_recv()

    def first_hop(which, h):
        arrived(which, h)
        to_up(which, h, t, h).start()
        to_dn(which, h, t, h).start()
        to_sib(which, 0, t, h).start()

    def gather_x(use):
        use(t, 0)
        use(t, 1)
        for h in range(2):
            got(0, sib, h)
            use(sib, h)
        for h in range(2):
            if h == 1:
                first_hop(1, 0)
            got(0, dn, h)
            to_sib(0, 1, dn, h).start()
            got(0, up, h)
            to_sib(0, 2, up, h).start()
            if h == 1:
                first_hop(1, 1)
            use(dn, h)
            use(up, h)
            arrived(2, h)
            to_sib(0, 3, far, h).start()
            use(far, h)
            for slot in (sdn, sup, sfar):
                got(0, slot, h)
                use(slot, h)

    def quarter(slot, h, q, send, recv, to):
        ref = gs.at[slot * 2 + h, :, q * uq : (q + 1) * uq]
        return remote(ref, ref, send, recv, e, to)

    def far_ring(slot, h, q):
        return quarter(slot, h, q, fr_send.at[h, q], fr_recv.at[h, q], (up, dn)[h])

    def far_core(slot, h, q):
        return quarter(slot, h, q, fc_send.at[h, q], fc_recv.at[h, q], sib)

    def gather_g(use, use_far):
        use(t, 0)
        use(t, 1)
        for h in range(2):
            got(1, sib, h)
            use(sib, h)
        got(1, dn, 0)
        for q in range(2):
            far_ring(dn, 0, q).start()
        to_sib(1, 1, dn, 0).start()
        got(1, up, 0)
        to_sib(1, 2, up, 0).start()
        use(dn, 0)
        use(up, 0)
        for slot in (sdn, sup):
            got(1, slot, 0)
            use(slot, 0)
        got(1, up, 1)
        for q in range(2):
            far_ring(up, 1, q).start()
        to_sib(1, 2, up, 1).start()
        got(1, dn, 1)
        to_sib(1, 1, dn, 1).start()
        use(dn, 1)
        use(up, 1)
        for slot in (sdn, sup):
            got(1, slot, 1)
            use(slot, 1)
        for q in range(2):
            for h in range(2):
                far_ring(far, h, q).wait_recv()
                far_core(far, h, q).start()
                use_far(far, h, q)
            for h in range(2):
                far_core(sfar, h, q).wait_recv()
                use_far(sfar, h, q)

    def sent(which):
        for n in range(2):
            to_up(which, n, t, 0).wait_send()
            to_dn(which, n, t, 0).wait_send()
        for n in range(4 - which):
            for h in range(2):
                to_sib(which, n, t, h).wait_send()

    def columns(slot):
        return pl.ds(pl.multiple_of(slot * width, width), width)

    def ucolumns(u):
        return pl.ds(pl.multiple_of(u * uw, uw), uw)

    def use_x(slot, h):
        u = slot * 2 + h

        def one(i, c):
            r = pl.ds(pl.multiple_of(i * tile, tile), tile)
            ab[:, r] += dot(wi[:, ucolumns(u)], xs[u, r, :], LAST)
            return c

        lax.fori_loop(0, rows // tile, one, 0)

    def send_out(u, q):
        w = pl.ds(pl.multiple_of(u * uw + q * uq, uq), uq)
        return remote(
            own_out.at[u, :, q * uq : (q + 1) * uq],
            grad_out.at[:, w],
            eo_send.at[u, q],
            eo_recv.at[u, q],
            other,
            t,
        )

    def send_in(u):
        return remote(
            own_in.at[u], grad_in.at[:, ucolumns(u)], ei_send.at[u], ei_recv.at[u], other, t
        )

    def use_g(slot, h):
        u = slot * 2 + h
        own_out[u] = dot(hid[...], gs[u], ROWS).astype(BF16)
        for q in range(2):
            send_out(u, q).start()

        def one(i, c):
            r = pl.ds(pl.multiple_of(i * tile, tile), tile)
            dh[:, r] += dot(wo[:, ucolumns(u)], gs[u, r, :], LAST)
            return c

        lax.fori_loop(0, rows // tile, one, 0)

    def use_g_far(slot, h, q):
        u = slot * 2 + h
        w = slice(q * uq, (q + 1) * uq)
        own_out[u, :, w] = dot(hid[...], gs[u, :, w], ROWS).astype(BF16)
        send_out(u, q).start()
        cols = pl.ds(pl.multiple_of(u * uw + q * uq, uq), uq)

        def one(i, c):
            r = pl.ds(pl.multiple_of(i * tile, tile), tile)
            dh[:, r] += dot(wo[:, cols], gs[u, r, w], LAST)
            return c

        lax.fori_loop(0, rows // tile, one, 0)

    first_hop(0, 0)
    dispatch(2, 0)
    dispatch(2, 1)
    first_hop(0, 1)
    load_og.wait()
    pack_rows(og, pack_g, gs, t, True)
    load_wi.wait()
    load_wo.wait()
    dispatch(1, 0)
    dispatch(1, 1)
    gather_x(use_x)

    def act(i, c):
        r = pl.ds(pl.multiple_of(i * lane, lane), lane)
        a, b = ab[0:ff, r], ab[ff : 2 * ff, r]
        hid[:, r] = (a * jax.nn.sigmoid(a) * b).astype(BF16)
        return c

    lax.fori_loop(0, rows // lane, act, 0)
    gather_g(use_g, use_g_far)

    def act_grad(i, c):
        r = pl.ds(pl.multiple_of(i * lane, lane), lane)
        a, b, d = ab[0:ff, r], ab[ff : 2 * ff, r], dh[:, r]
        s = jax.nn.sigmoid(a)
        da = d * b * s * (1.0 + a * (1.0 - s))
        db = d * (a * s)
        dadb_t[0:ff, r] = da.astype(BF16)
        dadb_t[ff : 2 * ff, r] = db.astype(BF16)
        dadb[r, :] = jnp.concatenate([da, db], axis=0).T.astype(BF16)
        return c

    lax.fori_loop(0, rows // lane, act_grad, 0)

    def wgrad_in(u):
        own_in[u] = dot(dadb_t[...], xs[u], ROWS).astype(BF16)
        send_in(u).start()

    def term(slot, dst, at):
        def one(i, c):
            r = pl.ds(pl.multiple_of(i * tile, tile), tile)
            dst[at, r, :] = dot(dadb[r, :], wi[:, columns(slot)], ROWS).astype(BF16)
            return c

        lax.fori_loop(0, rows // tile, one, 0)

    def send_part(at):
        return remote(part_sib.at[at], part_rec.at[at], p_send.at[at], p_recv.at[at], e, sib)

    def add(ref, at, src, src_at, h):
        r = pl.ds(h * half, half)
        ref[at, r, :] = (ref[at, r, :].astype(F32) + src[src_at, r, :].astype(F32)).astype(BF16)

    def chip(at):
        send_part(at).wait_recv()
        for h in range(2):
            add(part, at, part_rec, at, h)

    lower, upper = pl.ds(0, half), pl.ds(half, half)
    far_dn = remote(
        part.at[y_far, lower], half_rec.at[0, lower], h_send.at[0], h_recv.at[0], e, dn
    )
    far_up = remote(
        part.at[y_far, upper], half_rec.at[0, upper], h_send.at[1], h_recv.at[1], e, up
    )

    def full(direction, h):
        r = (lower, upper)[h]
        at, to = ((y_dn, dn), (y_up, up))[direction]
        return remote(
            part.at[at, r],
            full_rec.at[direction, r],
            f_send.at[direction, h],
            f_recv.at[direction, h],
            e,
            to,
        )

    def term_sib(slot, at):
        term(slot, part_sib, at)
        send_part(at).start()

    wgrad_in(0)
    wgrad_in(1)
    term_sib(sfar, y_far)
    term(far, part, y_far)
    term_sib(sdn, y_dn)
    term_sib(sup, y_up)
    chip(y_far)
    far_dn.start()
    far_up.start()
    wgrad_in(2)
    wgrad_in(3)
    term(dn, part, y_dn)
    term(up, part, y_up)
    chip(y_dn)
    full(0, 1).start()
    chip(y_up)
    full(1, 0).start()
    wgrad_in(4)
    wgrad_in(5)
    term_sib(sib, y)
    wgrad_in(6)
    wgrad_in(7)
    term(t, part, y)
    for u in range(8, 12):
        wgrad_in(u)
    far_dn.wait_recv()
    add(part, y_dn, half_rec, 0, 0)
    full(0, 0).start()
    far_up.wait_recv()
    add(part, y_up, half_rec, 0, 1)
    full(1, 1).start()
    for u in range(12, 16):
        wgrad_in(u)
    send_part(y).wait_recv()

    for h in range(2):
        full(0, h).wait_recv()
        full(1, h).wait_recv()

    def total(i, c):
        r = block(i)
        mine = part[y, r, :].astype(F32) + part_rec[y, r, :].astype(F32)
        ring = full_rec[0, r, :].astype(F32) + full_rec[1, r, :].astype(F32)
        part[y, r, :] = (mine + ring).astype(BF16)
        return c

    lax.fori_loop(0, n_ep, total, 0)

    def along_z(r, at, bx):
        to = lax.rem(z + r, n_z)
        return remote(
            part.at[y, block(bx * n_z + to)],
            back.at[bx, at],
            z_send.at[r, bx],
            z_recv.at[at, bx],
            x * n_z + to,
            t,
        )

    def send_z(r, c):
        for bx in range(n_x):
            along_z(r, z, bx).start()
        return c

    lax.fori_loop(1, n_z, send_z, 0)
    for bx in range(n_x):
        back[bx, z] = part[y, block(bx * n_z + z), :]

    def merge_out(u, c):
        for q in range(2):
            send_out(u, q).wait_recv()
        w = ucolumns(u)
        grad_out[:, w] = (grad_out[:, w].astype(F32) + own_out[u].astype(F32)).astype(BF16)
        return c

    lax.fori_loop(0, n_unit, merge_out, 0)

    def got_code(r, c):
        code_copy(r, lax.rem(x + r, n_x)).wait_recv()
        return c

    lax.fori_loop(1, n_x, got_code, 0)

    def got_z(r, c):
        for bx in range(n_x):
            along_z(r, lax.rem(z + r, n_z), bx).wait_recv()
        return c

    lax.fori_loop(1, n_z, got_z, 0)

    def along_x(r, at):
        to = lax.rem(x + r, n_x)
        return remote(
            token_sum.at[to], token_rec.at[at], c_send.at[1, r], c_recv.at[1, at], to * n_z + z, t
        )

    def by_token(r, c):
        bx = lax.rem(x + r, n_x)
        hot = jnp.concatenate([place(bx, x * n_z + k) for k in range(n_z)], axis=0).astype(BF16)
        returned = jnp.concatenate([back[bx, k] for k in range(n_z)], axis=0)
        token_sum[bx] = dot(hot, returned, FIRST).astype(BF16)
        return c

    def send_x(r, c):
        by_token(r, c)
        along_x(r, x).start()
        return c

    lax.fori_loop(1, n_x, send_x, 0)
    by_token(0, 0)
    token_rec[x] = token_sum[x]

    def got_x(r, c):
        along_x(r, lax.rem(x + r, n_x)).wait_recv()
        return c

    lax.fori_loop(1, n_x, got_x, 0)
    in_grad[...] = jnp.sum(token_rec[...].astype(F32), axis=0).astype(BF16)

    def end_peers(r, c):
        j = peer(r)
        for which in range(3):
            for h in range(2):
                rows_copy(which, h, j, e).wait_send()
        return c

    lax.fori_loop(1, n_ep, end_peers, 0)

    def end_z(r, c):
        for bx in range(n_x):
            along_z(r, z, bx).wait_send()
        return c

    lax.fori_loop(1, n_z, end_z, 0)

    def end_x(r, c):
        code_copy(r, x).wait_send()
        along_x(r, x).wait_send()
        return c

    lax.fori_loop(1, n_x, end_x, 0)
    sent(0)
    sent(1)
    tokens_far.wait_send()
    for h in range(2):
        for q in range(2):
            far_ring(far, h, q).wait_send()
            far_core(far, h, q).wait_send()
    far_dn.wait_send()
    far_up.wait_send()
    for direction in range(2):
        for h in range(2):
            full(direction, h).wait_send()

    def end_parts(at, c):
        send_part(at).wait_send()
        return c

    lax.fori_loop(0, n_y, end_parts, 0)

    def end_grads(u, c):
        for q in range(2):
            send_out(u, q).wait_send()
        return c

    lax.fori_loop(0, n_unit, end_grads, 0)

    def merge_in(u, c):
        send_in(u).wait_recv()
        w = ucolumns(u)
        grad_in[:, w] = (grad_in[:, w].astype(F32) + own_in[u].astype(F32)).astype(BF16)
        send_in(u).wait_send()
        return c

    lax.fori_loop(0, n_unit, merge_in, 0)


def body(tokens, out_grad, routes, probs, w_in, w_out):
    n_ep = lax.axis_size("ep")
    n_tp = lax.axis_size("tp")
    n_y = n_tp // 2
    n_unit = 2 * n_tp
    n_z = math.isqrt(n_ep)
    n_x = n_ep // n_z
    ntok, top = routes.shape
    cap = 2 * ntok * top // n_ep
    rows = n_ep * cap
    width = tokens.shape[1]
    uw = width // 2
    ff = w_out.shape[1]
    depth = w_out.shape[2]
    dma = pltpu.SemaphoreType.DMA
    vmem = pl.BlockSpec(memory_space=pltpu.VMEM)
    anywhere = pl.BlockSpec(memory_space=pl.ANY)
    flops = 2 * rows * depth * ff * 8
    made = pl.pallas_call(
        functools.partial(kernel, n_ep, n_y),
        out_shape=(
            pltpu.VMEM((ntok, width), BF16),
            pltpu.VMEM((2 * ff, depth), BF16),
            pltpu.VMEM((ff, depth), BF16),
        ),
        in_specs=[anywhere, anywhere, vmem, vmem, anywhere, anywhere],
        out_specs=(vmem, vmem, vmem),
        scratch_shapes=[
            pltpu.VMEM((ntok, width), BF16),
            pltpu.VMEM((ntok, width), BF16),
            pltpu.VMEM((ntok, width), BF16),
            pltpu.VMEM((n_unit, rows, uw), BF16),
            pltpu.VMEM((n_unit, rows, uw), BF16),
            pltpu.VMEM((2 * ff, depth), BF16),
            pltpu.VMEM((ff, depth), BF16),
            pltpu.VMEM((n_ep, 2, cap, uw), BF16),
            pltpu.VMEM((n_ep, 2, cap, uw), BF16),
            pltpu.VMEM((n_ep, 2, cap, uw), BF16),
            pltpu.VMEM((rows, ntok), BF16),
            pltpu.VMEM((n_x, n_ep, ntok), F32),
            pltpu.VMEM((n_ep, ntok), F32),
            pltpu.VMEM((2 * ff, rows), F32),
            pltpu.VMEM((ff, rows), F32),
            pltpu.VMEM((ff, rows), BF16),
            pltpu.VMEM((2 * ff, rows), BF16),
            pltpu.VMEM((rows, 2 * ff), BF16),
            pltpu.VMEM((n_unit, ff, uw), BF16),
            pltpu.VMEM((n_unit, 2 * ff, uw), BF16),
            pltpu.VMEM((n_y, rows, width), BF16),
            pltpu.VMEM((n_y, rows, width), BF16),
            pltpu.VMEM((n_y, rows, width), BF16),
            pltpu.VMEM((1, rows, width), BF16),
            pltpu.VMEM((2, rows, width), BF16),
            pltpu.VMEM((n_x, n_z, cap, width), BF16),
            pltpu.VMEM((n_x, ntok, width), BF16),
            pltpu.VMEM((n_x, ntok, width), BF16),
            dma((4,)),
            dma((1,)),
            dma((1,)),
            dma((3, 2, n_ep)),
            dma((3, 2, n_ep)),
            dma((2, 2, 2)),
            dma((2, 4, 2)),
            dma((2, n_unit)),
            dma((2, 2)),
            dma((2, 2)),
            dma((2, 2)),
            dma((2, 2)),
            dma((n_unit, 2)),
            dma((n_unit, 2)),
            dma((n_unit,)),
            dma((n_unit,)),
            dma((n_y,)),
            dma((n_y,)),
            dma((2,)),
            dma((2,)),
            dma((2, 2)),
            dma((2, 2)),
            dma((n_z, n_x)),
            dma((n_z, n_x)),
            dma((2, n_x)),
            dma((2, n_x)),
        ],
        compiler_params=pltpu.CompilerParams(
            collective_id=0, has_side_effects=True, vmem_limit_bytes=56 * 1024 * 1024
        ),
        cost_estimate=pl.CostEstimate(
            flops=flops, bytes_accessed=4 * rows * depth, transcendentals=2 * rows * ff
        ),
    )(
        tokens,
        out_grad,
        routes.T,
        probs.T,
        w_in.reshape(2 * ff, depth),
        w_out.reshape(ff, depth),
    )
    in_grad, grad_in, grad_out = pl.pallas_call(
        store,
        out_shape=tuple(jax.ShapeDtypeStruct(m.shape, BF16) for m in made),
        in_specs=[anywhere] * 3,
        out_specs=(anywhere,) * 3,
        scratch_shapes=[dma((3,))],
        compiler_params=pltpu.CompilerParams(vmem_limit_bytes=1024 * 1024),
    )(*(pltpu.with_memory_space_constraint(m, pltpu.VMEM) for m in made))
    return in_grad, grad_in.reshape(1, 2, ff, depth), grad_out.reshape(1, ff, depth)


def solution(mesh):
    return jax.shard_map(
        body,
        mesh=mesh,
        in_specs=(
            P("ep", "tp"),
            P("ep", "tp"),
            P("ep", None),
            P("ep", None),
            P("ep", None, "tp", None),
            P("ep", "tp", None),
        ),
        out_specs=(P("ep", "tp"), P("ep", None, "tp", None), P("ep", "tp", None)),
        check_vma=False,
    )
```

```python
import functools
import math

import jax
import jax.numpy as jnp
from jax import lax
from jax.experimental import pallas as pl
from jax.experimental.pallas import tpu as pltpu
from jax.sharding import PartitionSpec as P

BF16 = jnp.bfloat16
F32 = jnp.float32
LAST = (((1,), (1,)), ((), ()))
FIRST = (((0,), (0,)), ((), ()))
ROWS = (((1,), (0,)), ((), ()))


def dot(a, b, dims):
    return lax.dot_general(a, b, dims, preferred_element_type=F32)


def store(in_grad, grad_in, grad_out, in_grad_hbm, grad_in_hbm, grad_out_hbm, sems):
    copies = [
        pltpu.make_async_copy(src, dst, sems.at[i])
        for i, (src, dst) in enumerate(
            ((grad_in, grad_in_hbm), (grad_out, grad_out_hbm), (in_grad, in_grad_hbm))
        )
    ]
    for copy in copies:
        copy.start()
    for copy in copies:
        copy.wait()


def kernel(
    n_ep,
    n_y,
    tok_hbm,
    og_hbm,
    routes,
    probs,
    w_in,
    w_out,
    in_grad,
    grad_in,
    grad_out,
    tok,
    tok_far,
    og,
    xs,
    gs,
    wi,
    wo,
    pack_x,
    pack_g,
    pack_far,
    onehot,
    codes,
    share,
    ab,
    dh,
    hid,
    dadb_t,
    dadb,
    own_out,
    own_in,
    part_sib,
    part_rec,
    part,
    half_rec,
    full_rec,
    back,
    token_sum,
    token_rec,
    load_sem,
    t_send,
    t_recv,
    a_send,
    a_recv,
    ring_send,
    core_send,
    g_recv,
    fr_send,
    fr_recv,
    fc_send,
    fc_recv,
    eo_send,
    eo_recv,
    ei_send,
    ei_recv,
    p_send,
    p_recv,
    h_send,
    h_recv,
    f_send,
    f_recv,
    z_send,
    z_recv,
    c_send,
    c_recv,
):
    n_unit, rows, uw = xs.shape
    cap = rows // n_ep
    half = rows // 2
    uq = uw // 2
    width = tok.shape[1]
    ntok = tok.shape[0]
    ff = wo.shape[0]
    tile = min(256, rows)
    lane = min(128, rows)
    e = lax.axis_index("ep")
    t = lax.axis_index("tp")
    y = t // 2
    core = t % 2
    sib = y * 2 + (1 - core)
    y_up = lax.rem(y + 1, n_y)
    y_far = lax.rem(y + 2, n_y)
    y_dn = lax.rem(y + n_y - 1, n_y)
    up, far, dn = (v * 2 + core for v in (y_up, y_far, y_dn))
    sup, sfar, sdn = (v * 2 + (1 - core) for v in (y_up, y_far, y_dn))
    n_z = math.isqrt(n_ep)
    n_x = n_ep // n_z
    x = e // n_z
    z = e % n_z
    other = lax.rem(e + n_ep // 2, n_ep)

    def remote(src, dst, send, recv, ep, tp):
        return pltpu.make_async_remote_copy(
            src_ref=src,
            dst_ref=dst,
            send_sem=send,
            recv_sem=recv,
            device_id=(ep, tp),
            device_id_type=pl.DeviceIdType.MESH,
        )

    def peer(r):
        return lax.rem(e + r, n_ep)

    def signal(ep, tp):
        pl.semaphore_signal(
            barrier, inc=1, device_id=(ep, tp), device_id_type=pl.DeviceIdType.MESH
        )

    barrier = pltpu.get_barrier_semaphore()

    def greet(r, c):
        signal(peer(r), t)
        return c

    lax.fori_loop(1, n_ep, greet, 0)
    for who in (sib, up, dn, far):
        signal(e, who)

    load_tok, load_og, load_wi, load_wo = (
        pltpu.make_async_copy(src, dst, load_sem.at[i])
        for i, (src, dst) in enumerate(((tok_hbm, tok), (og_hbm, og), (w_in, wi), (w_out, wo)))
    )
    load_tok.start()
    load_og.start()
    load_wi.start()
    load_wo.start()

    copy_ids = lax.broadcasted_iota(jnp.int32, (n_ep, ntok), 0)
    hits = jnp.zeros((n_ep, ntok), F32)
    weights = jnp.zeros((n_ep, ntok), F32)
    shares = probs[...].astype(F32)
    for k in range(routes.shape[0]):
        same = routes[k : k + 1, :] == copy_ids
        hits = jnp.where(same, 1.0, hits)
        weights = jnp.where(same, shares[k : k + 1, :], weights)
    before = (
        lax.broadcasted_iota(jnp.int32, (ntok, ntok), 0)
        < lax.broadcasted_iota(jnp.int32, (ntok, ntok), 1)
    )
    before = jnp.where(before, 1.0, 0.0).astype(BF16)
    codes[x] = jnp.where(hits > 0.5, dot(hits.astype(BF16), before, ROWS), -1.0)
    share[...] = weights
    slots = lax.broadcasted_iota(jnp.int32, (cap, ntok), 0).astype(F32)

    def place(block_x, c):
        return jnp.where(codes[block_x, pl.ds(c, 1), :] == slots, 1.0, 0.0)

    def block(c):
        return pl.ds(pl.multiple_of(c * cap, cap), cap)

    def weighted(c):
        return jnp.where(codes[x, pl.ds(c, 1), :] == slots, share[pl.ds(c, 1), :], 0.0)

    def pack_rows(source, pack, buf, slot, scaled):
        group = min(4, n_ep)
        for g in range(0, n_ep, group):
            hot = onehot[g * cap : (g + group) * cap, :]
            if scaled:
                hot = jnp.concatenate([weighted(g + k) for k in range(group)]).astype(BF16)
            made = dot(hot, source[...], ROWS).astype(BF16)
            for k in range(group):
                for h in range(2):
                    pack[g + k, h] = made[k * cap : (k + 1) * cap, h * uw : (h + 1) * uw]
        for h in range(2):
            buf[slot * 2 + h, block(e), :] = pack[e, h]

    packs, bufs, own = (pack_x, pack_g, pack_far), (xs, gs, xs), (t, t, far)

    def rows_copy(which, h, j, at):
        return remote(
            packs[which].at[j, h],
            bufs[which].at[own[which] * 2 + h, block(at)],
            a_send.at[which, h, j],
            a_recv.at[which, h, at],
            j,
            t,
        )

    def dispatch(which, h):
        def one(r, c):
            rows_copy(which, h, peer(r), e).start()
            return c

        lax.fori_loop(1, n_ep, one, 0)

    def arrived(which, h):
        def one(r, c):
            rows_copy(which, h, peer(r), peer(r)).wait_recv()
            return c

        lax.fori_loop(1, n_ep, one, 0)

    for c in range(n_ep):
        onehot[c * cap : (c + 1) * cap, :] = place(x, c).astype(BF16)
    load_tok.wait()
    pack_rows(tok, pack_x, xs, t, False)
    pl.semaphore_wait(barrier, n_ep - 1 + 4)
    tokens_far = remote(tok, tok_far, t_send.at[0], t_recv.at[0], e, far)
    tokens_far.start()
    dispatch(0, 0)
    dispatch(0, 1)

    def code_copy(r, at):
        to = lax.rem(x + r, n_x)
        return remote(
            codes.at[x], codes.at[at], c_send.at[0, r], c_recv.at[0, at], to * n_z + z, t
        )

    def send_code(r, c):
        code_copy(r, x).start()
        return c

    lax.fori_loop(1, n_x, send_code, 0)
    ab[...] = jnp.zeros_like(ab)
    dh[...] = jnp.zeros_like(dh)
    tokens_far.wait_recv()
    pack_rows(tok_far, pack_far, xs, far, False)

    def unit(which, slot, h, send, to):
        ref = bufs[which].at[slot * 2 + h]
        return remote(ref, ref, send, g_recv.at[which, slot * 2 + h], e, to)

    def to_up(which, n, slot, h):
        return unit(which, slot, h, ring_send.at[which, 0, n], up)

    def to_dn(which, n, slot, h):
        return unit(which, slot, h, ring_send.at[which, 1, n], dn)

    def to_sib(which, n, slot, h):
        return unit(which, slot, h, core_send.at[which, n, h], sib)

    def got(which, slot, h):
        unit(which, slot, h, core_send.at[which, 0, h], sib).wait_recv()

    def first_hop(which, h):
        arrived(which, h)
        to_up(which, h, t, h).start()
        to_dn(which, h, t, h).start()
        to_sib(which, 0, t, h).start()

    def gather_x(use):
        use(t, 0)
        use(t, 1)
        for h in range(2):
            got(0, sib, h)
            use(sib, h)
        for h in range(2):
            if h == 1:
                first_hop(1, 0)
            got(0, dn, h)
            to_sib(0, 1, dn, h).start()
            if h == 1:
                first_hop(1, 1)
            got(0, up, h)
            to_sib(0, 2, up, h).start()
            use(dn, h)
            use(up, h)
            arrived(2, h)
            to_sib(0, 3, far, h).start()
            use(far, h)
            for slot in (sdn, sup, sfar):
                got(0, slot, h)
                use(slot, h)

    def quarter(slot, h, q, send, recv, to):
        ref = gs.at[slot * 2 + h, :, q * uq : (q + 1) * uq]
        return remote(ref, ref, send, recv, e, to)

    def far_ring(slot, h, q):
        return quarter(slot, h, q, fr_send.at[h, q], fr_recv.at[h, q], (up, dn)[h])

    def far_core(slot, h, q):
        return quarter(slot, h, q, fc_send.at[h, q], fc_recv.at[h, q], sib)

    def gather_g(use, use_far):
        use(t, 0)
        use(t, 1)
        for h in range(2):
            got(1, sib, h)
            use(sib, h)
        got(1, dn, 0)
        for q in range(2):
            far_ring(dn, 0, q).start()
        to_sib(1, 1, dn, 0).start()
        got(1, up, 0)
        to_sib(1, 2, up, 0).start()
        use(dn, 0)
        use(up, 0)
        for slot in (sdn, sup):
            got(1, slot, 0)
            use(slot, 0)
        got(1, up, 1)
        for q in range(2):
            far_ring(up, 1, q).start()
        to_sib(1, 2, up, 1).start()
        got(1, dn, 1)
        to_sib(1, 1, dn, 1).start()
        use(dn, 1)
        use(up, 1)
        for slot in (sdn, sup):
            got(1, slot, 1)
            use(slot, 1)
        for q in range(2):
            for h in range(2):
                far_ring(far, h, q).wait_recv()
                far_core(far, h, q).start()
                use_far(far, h, q)
            for h in range(2):
                far_core(sfar, h, q).wait_recv()
                use_far(sfar, h, q)

    def sent(which):
        for n in range(2):
            to_up(which, n, t, 0).wait_send()
            to_dn(which, n, t, 0).wait_send()
        for n in range(4 - which):
            for h in range(2):
                to_sib(which, n, t, h).wait_send()

    def columns(slot):
        return pl.ds(pl.multiple_of(slot * width, width), width)

    def ucolumns(u):
        return pl.ds(pl.multiple_of(u * uw, uw), uw)

    def use_x(slot, h):
        u = slot * 2 + h

        def one(i, c):
            r = pl.ds(pl.multiple_of(i * tile, tile), tile)
            ab[:, r] += dot(wi[:, ucolumns(u)], xs[u, r, :], LAST)
            return c

        lax.fori_loop(0, rows // tile, one, 0)

    def send_out(u, q):
        w = pl.ds(pl.multiple_of(u * uw + q * uq, uq), uq)
        return remote(
            own_out.at[u, :, q * uq : (q + 1) * uq],
            grad_out.at[:, w],
            eo_send.at[u, q],
            eo_recv.at[u, q],
            other,
            t,
        )

    def send_in(u):
        return remote(
            own_in.at[u], grad_in.at[:, ucolumns(u)], ei_send.at[u], ei_recv.at[u], other, t
        )

    def use_g(slot, h):
        u = slot * 2 + h
        own_out[u] = dot(hid[...], gs[u], ROWS).astype(BF16)
        for q in range(2):
            send_out(u, q).start()

        def one(i, c):
            r = pl.ds(pl.multiple_of(i * tile, tile), tile)
            dh[:, r] += dot(wo[:, ucolumns(u)], gs[u, r, :], LAST)
            return c

        lax.fori_loop(0, rows // tile, one, 0)

    def use_g_far(slot, h, q):
        u = slot * 2 + h
        w = slice(q * uq, (q + 1) * uq)
        own_out[u, :, w] = dot(hid[...], gs[u, :, w], ROWS).astype(BF16)
        send_out(u, q).start()
        cols = pl.ds(pl.multiple_of(u * uw + q * uq, uq), uq)

        def one(i, c):
            r = pl.ds(pl.multiple_of(i * tile, tile), tile)
            dh[:, r] += dot(wo[:, cols], gs[u, r, w], LAST)
            return c

        lax.fori_loop(0, rows // tile, one, 0)

    first_hop(0, 0)
    dispatch(2, 0)
    dispatch(2, 1)
    first_hop(0, 1)
    load_og.wait()
    pack_rows(og, pack_g, gs, t, True)
    load_wi.wait()
    load_wo.wait()
    dispatch(1, 0)
    dispatch(1, 1)
    gather_x(use_x)

    def act(i, c):
        r = pl.ds(pl.multiple_of(i * lane, lane), lane)
        a, b = ab[0:ff, r], ab[ff : 2 * ff, r]
        hid[:, r] = (a * jax.nn.sigmoid(a) * b).astype(BF16)
        return c

    lax.fori_loop(0, rows // lane, act, 0)
    gather_g(use_g, use_g_far)

    def act_grad(i, c):
        r = pl.ds(pl.multiple_of(i * lane, lane), lane)
        a, b, d = ab[0:ff, r], ab[ff : 2 * ff, r], dh[:, r]
        s = jax.nn.sigmoid(a)
        da = d * b * s * (1.0 + a * (1.0 - s))
        db = d * (a * s)
        dadb_t[0:ff, r] = da.astype(BF16)
        dadb_t[ff : 2 * ff, r] = db.astype(BF16)
        dadb[r, :] = jnp.concatenate([da, db], axis=0).T.astype(BF16)
        return c

    lax.fori_loop(0, rows // lane, act_grad, 0)

    def wgrad_in(u):
        own_in[u] = dot(dadb_t[...], xs[u], ROWS).astype(BF16)
        send_in(u).start()

    def term(slot, dst, at):
        def one(i, c):
            r = pl.ds(pl.multiple_of(i * tile, tile), tile)
            dst[at, r, :] = dot(dadb[r, :], wi[:, columns(slot)], ROWS).astype(BF16)
            return c

        lax.fori_loop(0, rows // tile, one, 0)

    def send_part(at):
        return remote(part_sib.at[at], part_rec.at[at], p_send.at[at], p_recv.at[at], e, sib)

    def add(ref, at, src, src_at, h):
        r = pl.ds(h * half, half)
        ref[at, r, :] = (ref[at, r, :].astype(F32) + src[src_at, r, :].astype(F32)).astype(BF16)

    def chip(at):
        send_part(at).wait_recv()
        for h in range(2):
            add(part, at, part_rec, at, h)

    lower, upper = pl.ds(0, half), pl.ds(half, half)
    far_dn = remote(
        part.at[y_far, lower], half_rec.at[0, lower], h_send.at[0], h_recv.at[0], e, dn
    )
    far_up = remote(
        part.at[y_far, upper], half_rec.at[0, upper], h_send.at[1], h_recv.at[1], e, up
    )

    def full(direction, h):
        r = (lower, upper)[h]
        at, to = ((y_dn, dn), (y_up, up))[direction]
        return remote(
            part.at[at, r],
            full_rec.at[direction, r],
            f_send.at[direction, h],
            f_recv.at[direction, h],
            e,
            to,
        )

    def term_sib(slot, at):
        term(slot, part_sib, at)
        send_part(at).start()

    wgrad_in(0)
    wgrad_in(1)
    term_sib(sfar, y_far)
    term(far, part, y_far)
    term_sib(sdn, y_dn)
    term_sib(sup, y_up)
    chip(y_far)
    far_dn.start()
    far_up.start()
    wgrad_in(2)
    wgrad_in(3)
    term(dn, part, y_dn)
    term(up, part, y_up)
    chip(y_dn)
    full(0, 1).start()
    chip(y_up)
    full(1, 0).start()
    wgrad_in(4)
    wgrad_in(5)
    term_sib(sib, y)
    wgrad_in(6)
    wgrad_in(7)
    term(t, part, y)
    for u in range(8, 12):
        wgrad_in(u)
    far_dn.wait_recv()
    add(part, y_dn, half_rec, 0, 0)
    full(0, 0).start()
    far_up.wait_recv()
    add(part, y_up, half_rec, 0, 1)
    full(1, 1).start()
    for u in range(12, 16):
        wgrad_in(u)
    send_part(y).wait_recv()

    for h in range(2):
        full(0, h).wait_recv()
        full(1, h).wait_recv()

    def total(i, c):
        r = block(i)
        mine = part[y, r, :].astype(F32) + part_rec[y, r, :].astype(F32)
        ring = full_rec[0, r, :].astype(F32) + full_rec[1, r, :].astype(F32)
        part[y, r, :] = (mine + ring).astype(BF16)
        return c

    lax.fori_loop(0, n_ep, total, 0)

    def along_z(r, at, bx):
        to = lax.rem(z + r, n_z)
        return remote(
            part.at[y, block(bx * n_z + to)],
            back.at[bx, at],
            z_send.at[r, bx],
            z_recv.at[at, bx],
            x * n_z + to,
            t,
        )

    def send_z(r, c):
        for bx in range(n_x):
            along_z(r, z, bx).start()
        return c

    lax.fori_loop(1, n_z, send_z, 0)
    for bx in range(n_x):
        back[bx, z] = part[y, block(bx * n_z + z), :]

    def merge_out(u, c):
        for q in range(2):
            send_out(u, q).wait_recv()
        w = ucolumns(u)
        grad_out[:, w] = (grad_out[:, w].astype(F32) + own_out[u].astype(F32)).astype(BF16)
        return c

    lax.fori_loop(0, n_unit, merge_out, 0)

    def got_code(r, c):
        code_copy(r, lax.rem(x + r, n_x)).wait_recv()
        return c

    lax.fori_loop(1, n_x, got_code, 0)

    def got_z(r, c):
        for bx in range(n_x):
            along_z(r, lax.rem(z + r, n_z), bx).wait_recv()
        return c

    lax.fori_loop(1, n_z, got_z, 0)

    def along_x(r, at):
        to = lax.rem(x + r, n_x)
        return remote(
            token_sum.at[to], token_rec.at[at], c_send.at[1, r], c_recv.at[1, at], to * n_z + z, t
        )

    def by_token(r, c):
        bx = lax.rem(x + r, n_x)
        hot = jnp.concatenate([place(bx, x * n_z + k) for k in range(n_z)], axis=0).astype(BF16)
        returned = jnp.concatenate([back[bx, k] for k in range(n_z)], axis=0)
        token_sum[bx] = dot(hot, returned, FIRST).astype(BF16)
        return c

    def send_x(r, c):
        by_token(r, c)
        along_x(r, x).start()
        return c

    lax.fori_loop(1, n_x, send_x, 0)
    by_token(0, 0)
    token_rec[x] = token_sum[x]

    def got_x(r, c):
        along_x(r, lax.rem(x + r, n_x)).wait_recv()
        return c

    lax.fori_loop(1, n_x, got_x, 0)
    in_grad[...] = jnp.sum(token_rec[...].astype(F32), axis=0).astype(BF16)

    def end_peers(r, c):
        j = peer(r)
        for which in range(3):
            for h in range(2):
                rows_copy(which, h, j, e).wait_send()
        return c

    lax.fori_loop(1, n_ep, end_peers, 0)

    def end_z(r, c):
        for bx in range(n_x):
            along_z(r, z, bx).wait_send()
        return c

    lax.fori_loop(1, n_z, end_z, 0)

    def end_x(r, c):
        code_copy(r, x).wait_send()
        along_x(r, x).wait_send()
        return c

    lax.fori_loop(1, n_x, end_x, 0)
    sent(0)
    sent(1)
    tokens_far.wait_send()
    for h in range(2):
        for q in range(2):
            far_ring(far, h, q).wait_send()
            far_core(far, h, q).wait_send()
    far_dn.wait_send()
    far_up.wait_send()
    for direction in range(2):
        for h in range(2):
            full(direction, h).wait_send()

    def end_parts(at, c):
        send_part(at).wait_send()
        return c

    lax.fori_loop(0, n_y, end_parts, 0)

    def end_grads(u, c):
        for q in range(2):
            send_out(u, q).wait_send()
        return c

    lax.fori_loop(0, n_unit, end_grads, 0)

    def merge_in(u, c):
        send_in(u).wait_recv()
        w = ucolumns(u)
        grad_in[:, w] = (grad_in[:, w].astype(F32) + own_in[u].astype(F32)).astype(BF16)
        send_in(u).wait_send()
        return c

    lax.fori_loop(0, n_unit, merge_in, 0)


def body(tokens, out_grad, routes, probs, w_in, w_out):
    n_ep = lax.axis_size("ep")
    n_tp = lax.axis_size("tp")
    n_y = n_tp // 2
    n_unit = 2 * n_tp
    n_z = math.isqrt(n_ep)
    n_x = n_ep // n_z
    ntok, top = routes.shape
    cap = 2 * ntok * top // n_ep
    rows = n_ep * cap
    width = tokens.shape[1]
    uw = width // 2
    ff = w_out.shape[1]
    depth = w_out.shape[2]
    dma = pltpu.SemaphoreType.DMA
    vmem = pl.BlockSpec(memory_space=pltpu.VMEM)
    anywhere = pl.BlockSpec(memory_space=pl.ANY)
    flops = 2 * rows * depth * ff * 8
    made = pl.pallas_call(
        functools.partial(kernel, n_ep, n_y),
        out_shape=(
            pltpu.VMEM((ntok, width), BF16),
            pltpu.VMEM((2 * ff, depth), BF16),
            pltpu.VMEM((ff, depth), BF16),
        ),
        in_specs=[anywhere, anywhere, vmem, vmem, anywhere, anywhere],
        out_specs=(vmem, vmem, vmem),
        scratch_shapes=[
            pltpu.VMEM((ntok, width), BF16),
            pltpu.VMEM((ntok, width), BF16),
            pltpu.VMEM((ntok, width), BF16),
            pltpu.VMEM((n_unit, rows, uw), BF16),
            pltpu.VMEM((n_unit, rows, uw), BF16),
            pltpu.VMEM((2 * ff, depth), BF16),
            pltpu.VMEM((ff, depth), BF16),
            pltpu.VMEM((n_ep, 2, cap, uw), BF16),
            pltpu.VMEM((n_ep, 2, cap, uw), BF16),
            pltpu.VMEM((n_ep, 2, cap, uw), BF16),
            pltpu.VMEM((rows, ntok), BF16),
            pltpu.VMEM((n_x, n_ep, ntok), F32),
            pltpu.VMEM((n_ep, ntok), F32),
            pltpu.VMEM((2 * ff, rows), F32),
            pltpu.VMEM((ff, rows), F32),
            pltpu.VMEM((ff, rows), BF16),
            pltpu.VMEM((2 * ff, rows), BF16),
            pltpu.VMEM((rows, 2 * ff), BF16),
            pltpu.VMEM((n_unit, ff, uw), BF16),
            pltpu.VMEM((n_unit, 2 * ff, uw), BF16),
            pltpu.VMEM((n_y, rows, width), BF16),
            pltpu.VMEM((n_y, rows, width), BF16),
            pltpu.VMEM((n_y, rows, width), BF16),
            pltpu.VMEM((1, rows, width), BF16),
            pltpu.VMEM((2, rows, width), BF16),
            pltpu.VMEM((n_x, n_z, cap, width), BF16),
            pltpu.VMEM((n_x, ntok, width), BF16),
            pltpu.VMEM((n_x, ntok, width), BF16),
            dma((4,)),
            dma((1,)),
            dma((1,)),
            dma((3, 2, n_ep)),
            dma((3, 2, n_ep)),
            dma((2, 2, 2)),
            dma((2, 4, 2)),
            dma((2, n_unit)),
            dma((2, 2)),
            dma((2, 2)),
            dma((2, 2)),
            dma((2, 2)),
            dma((n_unit, 2)),
            dma((n_unit, 2)),
            dma((n_unit,)),
            dma((n_unit,)),
            dma((n_y,)),
            dma((n_y,)),
            dma((2,)),
            dma((2,)),
            dma((2, 2)),
            dma((2, 2)),
            dma((n_z, n_x)),
            dma((n_z, n_x)),
            dma((2, n_x)),
            dma((2, n_x)),
        ],
        compiler_params=pltpu.CompilerParams(
            collective_id=0, has_side_effects=True, vmem_limit_bytes=56 * 1024 * 1024
        ),
        cost_estimate=pl.CostEstimate(
            flops=flops, bytes_accessed=4 * rows * depth, transcendentals=2 * rows * ff
        ),
    )(
        tokens,
        out_grad,
        routes.T,
        probs.T,
        w_in.reshape(2 * ff, depth),
        w_out.reshape(ff, depth),
    )
    in_grad, grad_in, grad_out = pl.pallas_call(
        store,
        out_shape=tuple(jax.ShapeDtypeStruct(m.shape, BF16) for m in made),
        in_specs=[anywhere] * 3,
        out_specs=(anywhere,) * 3,
        scratch_shapes=[dma((3,))],
        compiler_params=pltpu.CompilerParams(vmem_limit_bytes=1024 * 1024),
    )(*(pltpu.with_memory_space_constraint(m, pltpu.VMEM) for m in made))
    return in_grad, grad_in.reshape(1, 2, ff, depth), grad_out.reshape(1, ff, depth)


def solution(mesh):
    return jax.shard_map(
        body,
        mesh=mesh,
        in_specs=(
            P("ep", "tp"),
            P("ep", "tp"),
            P("ep", None),
            P("ep", None),
            P("ep", None, "tp", None),
            P("ep", "tp", None),
        ),
        out_specs=(P("ep", "tp"), P("ep", None, "tp", None), P("ep", "tp", None)),
        check_vma=False,
    )
```
